32 devices in a mesh: fsdp: 32 (over z, y, x, core).
Axes of the slice: x: 2, y: 2, z: 4, core: 2. Of those that a mesh axis runs over, the one named last changes fastest.
Arguments:
- hidden: bfloat16 [32768, 768], P('fsdp'), may hold values from -6 to 6
- lengths: int32 [32], P('fsdp'), may hold values from 1 to 1024, 24576 in all
- norm_gain: bfloat16 [768], P('fsdp'), may hold values from 0.5 to 1.5
- in_w: bfloat16 [768, 3352], P('fsdp'), may hold values from -0.21875 to 0.21875
- conv_w: bfloat16 [4, 1792], P(None, 'fsdp'), may hold values from -3 to 3
- conv_b: bfloat16 [1792], P('fsdp'), may hold values from -3 to 3
- dt_bias: float32 [24], replicated, may hold values from -4 to 2
- a_log: float32 [24], replicated, may hold values from -5 to 2.5
- skip: float32 [24], replicated, may hold values from 0.5 to 1.5
- gate_gain: bfloat16 [1536], P('fsdp'), may hold values from 0.5 to 1.5
- out_w: bfloat16 [1536, 768], P('fsdp'), may hold values from -0.21875 to 0.21875
- cotangent: bfloat16 [32768, 768], P('fsdp'), may hold values from -6 to 6
Outputs:
- block_out: bfloat16 [32768, 768], P('fsdp')
- grad_hidden: float32 [32768, 768], P('fsdp')
- grad_norm_gain: float32 [768], P('fsdp')
- grad_in_w: float32 [768, 3352], P('fsdp')
- grad_conv_w: float32 [4, 1792], P(None, 'fsdp')
- grad_conv_b: float32 [1792], P('fsdp')
- grad_dt_bias: float32 [24], replicated
- grad_a_log: float32 [24], replicated
- grad_skip: float32 [24], replicated
- grad_gate_gain: float32 [1536], P('fsdp')
- grad_out_w: float32 [1536, 768], P('fsdp')
The draws below stay inside these ranges and needn't reach their ends.
All inputs are finite; a program needn't handle non-finite values. No bound on the sum of `lengths` on one device may be relied on, other than what follows from the above.
Results may differ from the reference program's by a relative error of at most 0.0099.
Values may be sent and summed in bfloat16 or wider, within the bound.
No kernel may reach another device: no remote copies, remote signals or barrier semaphores. Data moves between devices by JAX's collectives and lax.ppermute only.
A program may use at most 192 MiB of HBM per device.

```python
import math
import jax
import jax.numpy as jnp
import numpy as np
from jax import lax

D = 768
HEADS = 24
HEAD_DIM = 64
STATE = 128
CONV_K = 4
SEQ = 1024
D_INNER = 1536
CONV_CH = 1792
PROJ = 3352
SEQS = 32
TOKENS = 32768
N_FSDP = 32


def rapid_heads(key):
    ranking = jax.random.permutation(key, HEADS)
    return ranking < max(1, HEADS // 8)


def draw_a_log(key, part):
    chosen = rapid_heads(key)
    key = jax.random.fold_in(key, 11)
    slow_key, rapid_key = jax.random.split(key)
    spread_rates = jax.random.uniform(slow_key, (HEADS,), jnp.float32, -5.0, 0.5)
    rapid_rates = jax.random.uniform(rapid_key, (HEADS,), jnp.float32, 2.0, 2.5)
    return jnp.where(chosen, rapid_rates, spread_rates)


def draw_dt_bias(key, part):
    chosen = rapid_heads(key)
    key = jax.random.fold_in(key, 23)
    slow_key, rapid_key = jax.random.split(key)
    spread_bias = jax.random.uniform(slow_key, (HEADS,), jnp.float32, -4.0, -1.0)
    rapid_bias = jax.random.uniform(rapid_key, (HEADS,), jnp.float32, 1.0, 2.0)
    return jnp.where(chosen, rapid_bias, spread_bias)


def steps_of(stream_key, dims, cuts, smallest, high):
    def one(dim, shards_of):
        heights = jax.random.uniform(jax.random.fold_in(jax.random.fold_in(stream_key, 6), dim), (shards_of,), jnp.float32, smallest / len(cuts), high / len(cuts))
        return jnp.repeat(jnp.exp(heights), dims[dim] // shards_of).reshape((-1,) + (1,) * (len(dims) - dim - 1))

    level = one(*cuts[0])
    for cut in cuts[1:]:
        level = level * one(*cut)
    return level


def split_up(amount, total, most, slope):
    weights = [(1 << 20) // math.isqrt(grade ** slope) + 1 for grade in range(2, amount + 1)]
    rest, holding = total - most - (amount - 1), [1] * (amount - 1)
    while rest > 0:
        free = [i for i in range(amount - 1) if holding[i] < most]
        mass, budget = sum([weights[i] for i in free]), rest
        for i in free:
            addition = min(most - holding[i], max(1, budget * weights[i] // mass), rest)
            holding[i] = holding[i] + addition
            rest = rest - addition
    return np.array([most] + holding)


def uneven_parts(stream_key, amount, total, bound, slope):
    if amount == 2:
        one = jax.random.randint(stream_key, (), max(1, total - bound), min(bound, total - 1) + 1)
        return jnp.stack([one, total - one])
    tallies = jnp.asarray(split_up(amount, total, bound, slope), jnp.int32)
    twos = (amount - 1) // 2
    giver, taker = tallies[1:1 + 2 * twos:2], tallies[2:2 + 2 * twos:2]
    slack = jnp.minimum(giver - 1, bound - taker)
    shifted = jax.random.randint(jax.random.fold_in(stream_key, 1), (twos,), 0, 1 << 20) % (slack + 1)
    tallies = tallies.at[1:1 + 2 * twos:2].set(giver - shifted).at[2:2 + 2 * twos:2].set(taker + shifted)
    return tallies[jax.random.permutation(jax.random.fold_in(stream_key, 2), amount)]


def centred(key, extent, deviation, reach, cuts=(), dtype=jnp.bfloat16):
    array = deviation * jax.random.normal(key, extent, jnp.float32)
    if cuts:
        array = array * steps_of(key, extent, cuts, -0.22, 0.18)
    return jnp.clip(array, -reach, reach).astype(dtype)


def setup_inputs(seed: int = 0) -> dict:
    seeds = jax.random.split(jax.random.key(seed), 13)
    hidden = centred(seeds[0], (TOKENS, D), 1.0, 6.0, ((0, 32),))
    lengths = uneven_parts(seeds[1], SEQS, SEQ * N_FSDP * 3 // 4, SEQ, 2).astype(jnp.int32)
    norm_gain = jnp.clip(1.0 + 0.1 * jax.random.normal(seeds[2], (D,), jnp.float32), 0.5, 1.5).astype(jnp.bfloat16)
    in_w = centred(seeds[3], (D, PROJ), D ** -0.5, 0.21875, ((0, 32),))
    conv_w = centred(seeds[4], (CONV_K, CONV_CH), CONV_K ** -0.5, 3.0, ((1, 32),))
    conv_b = centred(seeds[5], (CONV_CH,), 0.5, 3.0, ((0, 32),))
    dt_bias = draw_dt_bias(jax.random.fold_in(seeds[12], 71), 0)
    a_log = draw_a_log(jax.random.fold_in(seeds[12], 71), 0)
    skip = jnp.clip(jax.random.uniform(seeds[8], (HEADS,), jnp.float32, 0.5, 1.5), 0.5, 1.5)
    gate_gain = jnp.clip(1.0 + 0.1 * jax.random.normal(seeds[9], (D_INNER,), jnp.float32), 0.5, 1.5).astype(jnp.bfloat16)
    out_w = centred(seeds[10], (D_INNER, D), (D_INNER // 2) ** -0.5, 0.21875, ((0, 32),))
    cotangent = centred(seeds[11], (TOKENS, D), 1.0, 6.0, ((0, 32),))
    return dict(hidden=hidden, lengths=lengths, norm_gain=norm_gain, in_w=in_w, conv_w=conv_w, conv_b=conv_b, dt_bias=dt_bias, a_log=a_log, skip=skip, gate_gain=gate_gain, out_w=out_w, cotangent=cotangent)


@jax.custom_vjp
def low(v):
    return lax.optimization_barrier(v.astype(jnp.bfloat16)).astype(jnp.float32)

@jax.custom_vjp
def low_back(v):
    return v

def low_keep(v):
    return (low(v), None)

def low_pass(kept, grad):
    return (grad,)

def back_keep(v):
    return (v, None)

def back_low(kept, grad):
    return (low(grad),)
low.defvjp(low_keep, low_pass)
low_back.defvjp(back_keep, back_low)
eps = 1e-05
precise = lax.Precision.HIGHEST

def rms_scale(values_in, gain_row):
    return values_in * lax.rsqrt(lax.optimization_barrier(jnp.mean(values_in * values_in, axis=-1, keepdims=True)) + eps) * gain_row

def sequence_block(rows, row_mask, params):
    norm_gain, in_w, conv_w, conv_b, dt_bias, a_log, skip, gate_gain, out_w = params
    length = rows.shape[0]
    inner_width = HEADS * HEAD_DIM
    channels = inner_width + 2 * STATE
    normed = low(rms_scale(rows, norm_gain))
    projected = low_back(jnp.dot(normed, in_w, precision=precise))
    gate_z = projected[:, :inner_width]
    conv_in = projected[:, inner_width:inner_width + channels]
    dt_raw = projected[:, inner_width + channels:]
    padded = jnp.pad(conv_in, ((CONV_K - 1, 0), (0, 0)))
    conv_out = conv_b[None, :] + jnp.zeros((length, channels), jnp.float32)
    for offset in range(CONV_K):
        conv_out = conv_out + conv_w[offset][None, :] * padded[offset:offset + length]
    mixed = low(jax.nn.silu(conv_out))
    values = mixed[:, :inner_width].reshape(length, HEADS, HEAD_DIM)
    b_in = mixed[:, inner_width:inner_width + STATE]
    c_out = mixed[:, inner_width + STATE:]
    step_size = jax.nn.softplus(dt_raw + dt_bias[None, :])
    log_decay = -jnp.exp(a_log)[None, :] * step_size
    running = jnp.cumsum(log_decay, axis=0)
    places = jnp.arange(length)
    causal = (places[:, None] >= places[None, :])[:, :, None]
    differ = running[:, None, :] - running[None, :, :]
    decays = jnp.exp(jnp.where(causal, differ, -jnp.inf))
    intersection = jnp.dot(c_out, b_in.T, precision=precise)
    mixing = intersection[:, :, None] * decays * step_size[None, :, :]
    ssd = jnp.einsum('tsh,shp->thp', mixing, values, precision=precise) + skip[None, :, None] * values
    gated = ssd.reshape(length, inner_width) * jax.nn.silu(gate_z)
    normed_out = low(rms_scale(gated, gate_gain))
    branch = jnp.dot(normed_out, out_w, precision=precise)
    return row_mask[:, None] * (rows + branch)

def reference(hidden, lengths, norm_gain, in_w, conv_w, conv_b, dt_bias, a_log, skip, gate_gain, out_w, cotangent):
    inputs = hidden.astype(jnp.float32).reshape(N_FSDP, SEQ, D)
    positions = jnp.arange(SEQ).astype(jnp.int32)
    row_masks = (positions[None, :] < lengths[:, None]).astype(jnp.float32)
    params = (norm_gain.astype(jnp.float32), in_w.astype(jnp.float32), conv_w.astype(jnp.float32), conv_b.astype(jnp.float32), dt_bias, a_log, skip, gate_gain.astype(jnp.float32), out_w.astype(jnp.float32))

    def forward(rows_all, weights):

        def one_sequence(pieces):
            return sequence_block(pieces[0], pieces[1], weights)
        return lax.map(jax.checkpoint(one_sequence), (rows_all, row_masks))
    result, pullback = jax.vjp(forward, inputs, params)
    d_inputs, d_params = pullback(cotangent.astype(jnp.float32).reshape(N_FSDP, SEQ, D))
    return (result.reshape(TOKENS, D).astype(jnp.bfloat16), d_inputs.reshape(TOKENS, D), d_params[0], d_params[1], d_params[2], d_params[3], d_params[4], d_params[5], d_params[6], d_params[7], d_params[8])
```

```python
import functools

import jax
import jax.numpy as jnp
from jax import lax
from jax.experimental import pallas as pl
from jax.experimental.pallas import tpu as pltpu
from jax.sharding import PartitionSpec as P

HEADS = 24
HEAD_DIM = 64
STATE = 128
CONV_K = 4
INNER = HEADS * HEAD_DIM
CHANNELS = INNER + 2 * STATE
LANES = 128
CHUNK = 128
PAIRS = HEADS // 2
VMEM_BYTES = 56 * 1024 * 1024
EPS = 1e-05
F32 = jnp.float32
BF16 = jnp.bfloat16
HIGHEST = lax.Precision.HIGHEST


def mm(a, b):
    return lax.dot_general(a, b, (((1,), (0,)), ((), ())), preferred_element_type=F32)


def mm_bt(a, b):
    return lax.dot_general(a, b, (((1,), (1,)), ((), ())), preferred_element_type=F32)


def mm_at(a, b):
    return lax.dot_general(a, b, (((0,), (0,)), ((), ())), preferred_element_type=F32)


def sigmoid(x):
    return 0.5 * jnp.tanh(0.5 * x) + 0.5


def split_two(v):
    high = v.astype(BF16)
    low = (v - high.astype(F32)).astype(BF16)
    return high, low


def widen(v, spread):
    high, low = split_two(jnp.where(lane_is_head(), v, 0.0))
    packed = high.astype(F32) + pltpu.roll(low.astype(F32), 64, 1)
    return mm(packed.astype(BF16), spread)


def head_sums(v, gather):
    high, low = split_two(v)
    return mm(high, gather) + mm(low, gather)


def lane_is_head():
    return lax.broadcasted_iota(jnp.int32, (1, LANES), 1) < HEADS


def triangle(kind):
    rows = lax.broadcasted_iota(jnp.int32, (CHUNK, CHUNK), 0)
    columns = lax.broadcasted_iota(jnp.int32, (CHUNK, CHUNK), 1)
    return rows >= columns if kind == "lower" else rows <= columns


def forward_kernel(
    hidden_ref, gain_ref, wc_ref, wdt_ref, cw_ref, cb_ref, dtb_ref, alog_ref, skip_ref, spread_ref,
    normed_ref, mixed_ref, slope_ref, convin_ref, step_ref, run_ref, sig_ref, ssd_ref, enter_ref,
    tail, state,
):
    first = pl.program_id(0) == 0

    @pl.when(first)
    def _():
        tail[0:8, :] = jnp.zeros((8, CHANNELS), F32)
        state[...] = jnp.zeros_like(state)

    x = hidden_ref[...].astype(F32)
    scale = lax.rsqrt(jnp.mean(x * x, axis=-1, keepdims=True) + EPS)
    normed = (x * scale * gain_ref[...]).astype(BF16)
    normed_ref[...] = normed

    conv_in = mm(normed, wc_ref[...])
    convin_ref[...] = conv_in.astype(BF16)
    tail[8 : 8 + CHUNK, :] = conv_in
    conv_out = cb_ref[...] + cw_ref[3:4, :] * conv_in
    for k in range(CONV_K - 1):
        conv_out = conv_out + cw_ref[k : k + 1, :] * tail[5 + k : 5 + k + CHUNK, :]
    tail[0:8, :] = tail[CHUNK : CHUNK + 8, :]
    gate = sigmoid(conv_out)
    mixed = (conv_out * gate).astype(BF16)
    mixed_ref[...] = mixed
    slope_ref[...] = (gate * (1.0 + conv_out * (1.0 - gate))).astype(BF16)

    dt = mm(normed, wdt_ref[...]) + dtb_ref[...]
    step = jnp.where(lane_is_head(), jnp.maximum(dt, 0.0) + jnp.log1p(jnp.exp(-jnp.abs(dt))), 0.0)
    step_ref[...] = step
    sig_ref[...] = sigmoid(dt)
    log_decay = -jnp.exp(alog_ref[...]) * step
    lower = triangle("lower")
    run = jnp.dot(lower.astype(F32), log_decay, precision=HIGHEST, preferred_element_type=F32)
    run_ref[...] = run
    run_t = jnp.transpose(run)
    last = run[CHUNK - 1 : CHUNK, :]

    spread = spread_ref[...]
    values = mixed[:, :INNER].astype(F32)
    b_in = mixed[:, INNER : INNER + STATE]
    c_out = mixed[:, INNER + STATE :]
    scores = jnp.where(lower, mm_bt(c_out, b_in), 0.0)
    stepped = (widen(step, spread) * values).astype(BF16)
    entering = state[...]
    enter_low = entering.astype(BF16)
    enter_ref[0] = enter_low
    ssd_ref[...] = widen(jnp.exp(run), spread) * mm(c_out, enter_low) + skip_ref[...] * values
    to_end = (widen(jnp.exp(last - run), spread) * stepped.astype(F32)).astype(BF16)
    through = widen(jnp.broadcast_to(jnp.exp(last), (8, LANES)), spread)[0:1, :]
    state[...] = through * entering + mm_at(b_in, to_end)

    left_half = lax.broadcasted_iota(jnp.int32, (CHUNK, LANES), 1) < HEAD_DIM
    zero = jnp.zeros((CHUNK, LANES), BF16)
    for pair in range(PAIRS):
        mixing = []
        for h in (2 * pair, 2 * pair + 1):
            decay = jnp.exp(jnp.minimum(run[:, h : h + 1] - run_t[h : h + 1, :], 0.0))
            mixing.append((scores * decay).astype(BF16))
        both = stepped[:, pair * LANES : (pair + 1) * LANES]
        right = jnp.concatenate([jnp.where(left_half, both, zero), jnp.where(left_half, zero, both)], axis=0)
        ssd_ref[:, pair * LANES : (pair + 1) * LANES] += mm(jnp.concatenate(mixing, axis=1), right)


def forward(hidden, gain, wc, wdt, cw, cb, dtb, alog, skip_wide, spread):
    rows, width = hidden.shape
    chunks = rows // CHUNK
    whole = lambda a: pl.BlockSpec(a.shape, lambda i: (0,) * a.ndim)
    part = lambda n: pl.BlockSpec((CHUNK, n), lambda i: (i, 0))
    ins = (hidden, gain, wc, wdt, cw, cb, dtb, alog, skip_wide, spread)
    flops = 2 * rows * (width * (CHANNELS + LANES) + 3 * STATE * INNER + CHUNK * INNER * 2)
    return pl.pallas_call(
        forward_kernel,
        grid=(chunks,),
        in_specs=[part(width)] + [whole(a) for a in ins[1:]],
        out_specs=[
            part(width), part(CHANNELS), part(CHANNELS), part(CHANNELS), part(LANES), part(LANES), part(LANES), part(INNER),
            pl.BlockSpec((1, STATE, INNER), lambda i: (i, 0, 0)),
        ],
        out_shape=[
            jax.ShapeDtypeStruct((rows, width), BF16),
            jax.ShapeDtypeStruct((rows, CHANNELS), BF16),
            jax.ShapeDtypeStruct((rows, CHANNELS), BF16),
            jax.ShapeDtypeStruct((rows, CHANNELS), BF16),
            jax.ShapeDtypeStruct((rows, LANES), F32),
            jax.ShapeDtypeStruct((rows, LANES), F32),
            jax.ShapeDtypeStruct((rows, LANES), F32),
            jax.ShapeDtypeStruct((rows, INNER), F32),
            jax.ShapeDtypeStruct((chunks, STATE, INNER), BF16),
        ],
        scratch_shapes=[pltpu.VMEM((CHUNK + 8, CHANNELS), F32), pltpu.VMEM((STATE, INNER), F32)],
        compiler_params=pltpu.CompilerParams(dimension_semantics=("arbitrary",), vmem_limit_bytes=VMEM_BYTES),
        cost_estimate=pl.CostEstimate(flops=flops, bytes_accessed=30_000_000, transcendentals=0),
        name="ssd_forward",
    )(*ins)


def gate_kernel(
    keep_ref, normed_ref, ssd_ref, cot_ref, hidden_ref, wz_ref, wo_ref, gg_ref,
    out_ref, dz_ref, dssd_ref, no_ref, grow_ref, dgg_ref,
):
    @pl.when(pl.program_id(0) == 0)
    def _():
        dgg_ref[...] = jnp.zeros_like(dgg_ref)

    keep = keep_ref[:, 0:1]
    grow = (cot_ref[...].astype(F32) * keep).astype(BF16)
    grow_ref[...] = grow
    wo = wo_ref[...]
    gate_gain = gg_ref[...]
    z = mm(normed_ref[...], wz_ref[...])
    sig = sigmoid(z)
    silu = z * sig
    ssd = ssd_ref[...]
    gated = ssd * silu
    scale = lax.rsqrt(jnp.mean(gated * gated, axis=-1, keepdims=True) + EPS)
    unit = gated * scale
    out_low = (unit * gate_gain).astype(BF16)
    no_ref[...] = out_low
    out_ref[...] = (keep * (hidden_ref[...].astype(F32) + mm(out_low, wo))).astype(BF16)
    d_out = mm_bt(grow, wo)
    dgg_ref[...] += jnp.sum(d_out * unit, axis=0, keepdims=True)
    d_unit = d_out * gate_gain
    d_gated = scale * (d_unit - unit * jnp.mean(d_unit * unit, axis=-1, keepdims=True))
    dssd_ref[...] = d_gated * silu
    dz_ref[...] = (d_gated * ssd * (sig * (1.0 + z * (1.0 - sig)))).astype(BF16)


def gate(keep, normed, ssd, cot, hidden, wz, wo, gate_gain):
    rows, width = hidden.shape
    tile = 256
    whole = lambda a: pl.BlockSpec(a.shape, lambda i: (0,) * a.ndim)
    part = lambda n: pl.BlockSpec((tile, n), lambda i: (i, 0))
    return pl.pallas_call(
        gate_kernel,
        grid=(rows // tile,),
        in_specs=[part(LANES), part(width), part(INNER), part(width), part(width), whole(wz), whole(wo), whole(gate_gain)],
        out_specs=[part(width), part(INNER), part(INNER), part(INNER), part(width), pl.BlockSpec((1, INNER), lambda i: (0, 0))],
        out_shape=[
            jax.ShapeDtypeStruct((rows, width), BF16),
            jax.ShapeDtypeStruct((rows, INNER), BF16),
            jax.ShapeDtypeStruct((rows, INNER), F32),
            jax.ShapeDtypeStruct((rows, INNER), BF16),
            jax.ShapeDtypeStruct((rows, width), BF16),
            jax.ShapeDtypeStruct((1, INNER), F32),
        ],
        compiler_params=pltpu.CompilerParams(dimension_semantics=("arbitrary",), vmem_limit_bytes=VMEM_BYTES),
        cost_estimate=pl.CostEstimate(flops=2 * rows * width * INNER * 3, bytes_accessed=30_000_000, transcendentals=0),
        name="gate_both_ways",
    )(keep, normed, ssd, cot, hidden, wz, wo, gate_gain)


def backward_kernel(
    mixed_ref, slope_ref, convin_ref, step_ref, run_ref, sig_ref, ssd_ref, enter_ref, dssd_ref,
    cw_ref, alog_ref, skip_ref, spread_ref, gather_ref,
    dconv_ref, ddt_ref, dcw_ref, dcb_ref, dsmall_ref, dskip_ref,
    ahead, d_state, d_values,
):
    @pl.when(pl.program_id(0) == 0)
    def _():
        ahead[CHUNK : CHUNK + 8, :] = jnp.zeros((8, CHANNELS), F32)
        d_state[...] = jnp.zeros_like(d_state)
        dcw_ref[...] = jnp.zeros_like(dcw_ref)
        dcb_ref[...] = jnp.zeros_like(dcb_ref)
        dsmall_ref[...] = jnp.zeros_like(dsmall_ref)
        dskip_ref[...] = jnp.zeros_like(dskip_ref)

    spread = spread_ref[...]
    gather = gather_ref[...]
    step = step_ref[...]
    run = run_ref[...]
    run_t = jnp.transpose(run)
    last = run[CHUNK - 1 : CHUNK, :]
    skip = skip_ref[...]
    mixed = mixed_ref[...]
    values = mixed[:, :INNER].astype(F32)
    b_in = mixed[:, INNER : INNER + STATE]
    c_out = mixed[:, INNER + STATE :]
    step_wide = widen(step, spread)
    end_wide = widen(jnp.exp(last - run), spread)
    stepped = (step_wide * values).astype(BF16)
    to_end = (end_wide * stepped.astype(F32)).astype(BF16)
    through = widen(jnp.broadcast_to(jnp.exp(last), (8, LANES)), spread)[0:1, :]
    d_ssd = dssd_ref[...]
    d_low = d_ssd.astype(BF16)
    scaled = (widen(jnp.exp(run), spread) * d_low.astype(F32)).astype(BF16)
    entering = enter_ref[0]
    d_leave = d_state[...]
    d_leave_low = d_leave.astype(BF16)
    upper = triangle("upper")
    scores_t = jnp.where(upper, mm_bt(b_in, c_out), 0.0)

    left_half = lax.broadcasted_iota(jnp.int32, (CHUNK, LANES), 1) < HEAD_DIM
    zero = jnp.zeros((CHUNK, LANES), BF16)
    d_scores_t = jnp.zeros((CHUNK, CHUNK), F32)
    for pair in range(PAIRS):
        lanes = slice(pair * LANES, (pair + 1) * LANES)
        d_pair = d_low[:, lanes]
        x_pair = stepped[:, lanes]
        d_split = jnp.concatenate([jnp.where(left_half, d_pair, zero), jnp.where(left_half, zero, d_pair)], axis=0)
        d_mixing = mm_bt(x_pair, d_split)
        mixing = []
        for slot, h in enumerate((2 * pair, 2 * pair + 1)):
            decay = jnp.exp(jnp.minimum(run_t[h : h + 1, :] - run[:, h : h + 1], 0.0))
            d_scores_t = d_scores_t + d_mixing[:, slot * CHUNK : (slot + 1) * CHUNK] * decay
            mixing.append((scores_t * decay).astype(BF16))
        d_values[:, lanes] = mm(jnp.concatenate(mixing, axis=1), d_split)

    d_scores_t = jnp.where(upper, d_scores_t, 0.0).astype(BF16)
    d_c = mm_at(d_scores_t, b_in) + mm_bt(scaled, entering)
    d_b = mm(d_scores_t, c_out) + mm_bt(to_end, d_leave_low)
    from_state = mm(b_in, d_leave_low)
    d_state[...] = through * d_leave + mm_at(c_out, scaled)

    d_stepped = d_values[...]
    state_part = to_end.astype(F32) * from_state
    ssd = ssd_ref[...]
    flow = d_low.astype(F32) * (ssd - skip * values) - stepped.astype(F32) * d_stepped - state_part
    ending = jnp.sum(state_part, axis=0, keepdims=True) + through * jnp.sum(
        entering.astype(F32) * d_leave, axis=0, keepdims=True
    )
    is_last = lax.broadcasted_iota(jnp.int32, (CHUNK, 1), 0) == CHUNK - 1
    d_run = head_sums(flow + jnp.where(is_last, ending, 0.0), gather)
    d_stepped = d_stepped + end_wide * from_state
    d_step = head_sums(values * d_stepped, gather)
    dskip_ref[...] += jnp.sum(d_ssd * values, axis=0, keepdims=True)
    d_x = skip * d_ssd + step_wide * d_stepped

    rate = jnp.exp(alog_ref[...])
    d_log = jnp.dot(upper.astype(F32), d_run, precision=HIGHEST, preferred_element_type=F32)
    d_step = d_step - rate * d_log
    d_dt = jnp.where(lane_is_head(), d_step * sig_ref[...], 0.0)
    ddt_ref[...] = d_dt.astype(BF16)
    dsmall_ref[0:1, :] += jnp.sum(d_dt, axis=0, keepdims=True)
    dsmall_ref[1:2, :] -= rate * jnp.sum(d_log * step, axis=0, keepdims=True)

    slope = slope_ref[...].astype(F32)
    ahead[0:CHUNK, :INNER] = d_x * slope[:, :INNER]
    ahead[0:CHUNK, INNER : INNER + STATE] = d_b * slope[:, INNER : INNER + STATE]
    ahead[0:CHUNK, INNER + STATE :] = d_c * slope[:, INNER + STATE :]
    conv_in = convin_ref[...].astype(F32)
    total = jnp.zeros((CHUNK, CHANNELS), F32)
    for k in range(CONV_K):
        moved = ahead[CONV_K - 1 - k : CONV_K - 1 - k + CHUNK, :]
        total = total + cw_ref[k : k + 1, :] * moved
        dcw_ref[k : k + 1, :] += jnp.sum(moved * conv_in, axis=0, keepdims=True)
    dcb_ref[...] += jnp.sum(ahead[0:CHUNK, :], axis=0, keepdims=True)
    dconv_ref[...] = total.astype(BF16)
    ahead[CHUNK : CHUNK + 8, :] = ahead[0:8, :]


def backward(mixed, slope, convin, step, run, sig, ssd, enter, d_ssd, cw, alog, skip_wide, spread, gather):
    rows = mixed.shape[0]
    chunks = rows // CHUNK
    whole = lambda a: pl.BlockSpec(a.shape, lambda i: (0,) * a.ndim)
    part = lambda n: pl.BlockSpec((CHUNK, n), lambda i: (chunks - 1 - i, 0))
    total = lambda r, n: pl.BlockSpec((r, n), lambda i: (0, 0))
    flops = 2 * rows * (5 * STATE * INNER + CHUNK * INNER * 4)
    return pl.pallas_call(
        backward_kernel,
        grid=(chunks,),
        in_specs=[
            part(CHANNELS), part(CHANNELS), part(CHANNELS), part(LANES), part(LANES), part(LANES), part(INNER),
            pl.BlockSpec((1, STATE, INNER), lambda i: (chunks - 1 - i, 0, 0)), part(INNER),
        ] + [whole(a) for a in (cw, alog, skip_wide, spread, gather)],
        out_specs=[part(CHANNELS), part(LANES), total(CONV_K, CHANNELS), total(1, CHANNELS), total(8, LANES), total(1, INNER)],
        out_shape=[
            jax.ShapeDtypeStruct((rows, CHANNELS), BF16),
            jax.ShapeDtypeStruct((rows, LANES), BF16),
            jax.ShapeDtypeStruct((CONV_K, CHANNELS), F32),
            jax.ShapeDtypeStruct((1, CHANNELS), F32),
            jax.ShapeDtypeStruct((8, LANES), F32),
            jax.ShapeDtypeStruct((1, INNER), F32),
        ],
        scratch_shapes=[
            pltpu.VMEM((CHUNK + 8, CHANNELS), F32), pltpu.VMEM((STATE, INNER), F32), pltpu.VMEM((CHUNK, INNER), F32),
        ],
        compiler_params=pltpu.CompilerParams(dimension_semantics=("arbitrary",), vmem_limit_bytes=VMEM_BYTES),
        cost_estimate=pl.CostEstimate(flops=flops, bytes_accessed=40_000_000, transcendentals=0),
        name="ssd_backward",
    )(mixed, slope, convin, step, run, sig, ssd, enter, d_ssd, cw, alog, skip_wide, spread, gather)


def entry_kernel(hidden_ref, grow_ref, dz_ref, dconv_ref, ddt_ref, gain_ref, wz_ref, wc_ref, wdt_ref, gh_ref, dgain_ref):
    @pl.when(pl.program_id(0) == 0)
    def _():
        dgain_ref[...] = jnp.zeros_like(dgain_ref)

    x = hidden_ref[...].astype(F32)
    scale = lax.rsqrt(jnp.mean(x * x, axis=-1, keepdims=True) + EPS)
    unit = x * scale
    d_normed = mm_bt(dz_ref[...], wz_ref[...]) + mm_bt(dconv_ref[...], wc_ref[...]) + mm_bt(ddt_ref[...], wdt_ref[...])
    dgain_ref[...] += jnp.sum(d_normed * unit, axis=0, keepdims=True)
    d_unit = d_normed * gain_ref[...]
    d_x = scale * (d_unit - unit * jnp.mean(d_unit * unit, axis=-1, keepdims=True))
    gh_ref[...] = grow_ref[...].astype(F32) + d_x


def entry(hidden, grow, dz, dconv, ddt, gain, wz, wc, wdt):
    rows, width = hidden.shape
    tile = 256
    whole = lambda a: pl.BlockSpec(a.shape, lambda i: (0,) * a.ndim)
    part = lambda n: pl.BlockSpec((tile, n), lambda i: (i, 0))
    return pl.pallas_call(
        entry_kernel,
        grid=(rows // tile,),
        in_specs=[part(width), part(width), part(INNER), part(CHANNELS), part(LANES)] + [whole(a) for a in (gain, wz, wc, wdt)],
        out_specs=[part(width), pl.BlockSpec((1, width), lambda i: (0, 0))],
        out_shape=[jax.ShapeDtypeStruct((rows, width), F32), jax.ShapeDtypeStruct((1, width), F32)],
        compiler_params=pltpu.CompilerParams(dimension_semantics=("arbitrary",), vmem_limit_bytes=VMEM_BYTES),
        cost_estimate=pl.CostEstimate(flops=2 * rows * width * (INNER + CHANNELS + LANES), bytes_accessed=20_000_000, transcendentals=0),
        name="input_norm_backward",
    )(hidden, grow, dz, dconv, ddt, gain, wz, wc, wdt)


def pad_lanes(v):
    return jnp.pad(v, [(0, 0)] * (v.ndim - 1) + [(0, LANES - v.shape[-1])])


def head_maps():
    lane = jnp.arange(INNER)[None, :] // HEAD_DIM
    row = jnp.arange(LANES)[:, None]
    spread = (lane == row % 64).astype(BF16)
    gather = (lane == row).astype(BF16).T
    return spread, gather


def contract_rows(left, right):
    return lax.dot_general(left, right, (((0,), (0,)), ((), ())), preferred_element_type=F32)


def block(hidden, lengths, full_norm, full_in, full_conv, full_bias, dt_bias, a_log, skip, full_gate, full_out, cotangent):
    length = hidden.shape[0]
    spread, gather = head_maps()
    gain = full_norm.astype(F32)[None, :]
    wz = full_in[:, :INNER]
    wc = full_in[:, INNER : INNER + CHANNELS]
    wdt = pad_lanes(full_in[:, INNER + CHANNELS :])
    cw = full_conv.astype(F32)
    cb = full_bias.astype(F32)[None, :]
    dtb = pad_lanes(dt_bias[None, :])
    alog = pad_lanes(a_log[None, :])
    skip_wide = jnp.repeat(skip, HEAD_DIM)[None, :]
    keep = jnp.broadcast_to((jnp.arange(length) < lengths[0]).astype(F32)[:, None], (length, LANES))
    normed, mixed, slope, convin, step, run, sig, ssd, enter = forward(
        hidden, gain, wc, wdt, cw, cb, dtb, alog, skip_wide, spread
    )
    block_out, dz, d_ssd, out_low, grow, d_gate = gate(
        keep, normed, ssd, cotangent, hidden, wz, full_out, full_gate.astype(F32)[None, :]
    )
    d_out_w = contract_rows(out_low, grow)
    dconv, ddt, dcw, dcb, dsmall, dskip = backward(
        mixed, slope, convin, step, run, sig, ssd, enter, d_ssd, cw, alog, skip_wide, spread, gather
    )
    grad_hidden, d_gain = entry(hidden, grow, dz, dconv, ddt, gain, wz, wc, wdt)
    d_in_w = jnp.concatenate(
        [contract_rows(normed, dz), contract_rows(normed, dconv), contract_rows(normed, ddt)[:, :HEADS]], axis=1
    )
    d_skip = dskip.reshape(HEADS, HEAD_DIM).sum(1)
    return (block_out, grad_hidden, d_gain[0], d_in_w, dcw, dcb[0], dsmall[0, :HEADS], dsmall[1, :HEADS], d_skip, d_gate[0], d_out_w)


def local(hidden, lengths, norm_gain, in_w, conv_w, conv_b, dt_bias, a_log, skip, gate_gain, out_w, cotangent):
    full_norm, full_in, full_conv, full_bias, full_gate, full_out = (
        lax.all_gather(norm_gain, "fsdp", axis=0, tiled=True),
        lax.all_gather(in_w, "fsdp", axis=0, tiled=True),
        lax.all_gather(conv_w, "fsdp", axis=1, tiled=True),
        lax.all_gather(conv_b, "fsdp", axis=0, tiled=True),
        lax.all_gather(gate_gain, "fsdp", axis=0, tiled=True),
        lax.all_gather(out_w, "fsdp", axis=0, tiled=True),
    )
    outs = block(
        hidden, lengths, full_norm, full_in, full_conv, full_bias, dt_bias, a_log, skip, full_gate, full_out, cotangent
    )
    block_out, grad_hidden, d_gain, d_in, d_cw, d_cb, d_dtb, d_alog, d_skip, d_gate, d_out = outs
    scatter = functools.partial(lax.psum_scatter, axis_name="fsdp", tiled=True)
    head_sums = lax.psum((d_dtb, d_alog, d_skip), "fsdp")
    return (
        block_out, grad_hidden, scatter(d_gain, scatter_dimension=0), scatter(d_in, scatter_dimension=0),
        scatter(d_cw, scatter_dimension=1), scatter(d_cb, scatter_dimension=0), *head_sums,
        scatter(d_gate, scatter_dimension=0), scatter(d_out, scatter_dimension=0),
    )


def solution(mesh):
    rows, split, none = P("fsdp", None), P("fsdp"), P()
    columns = P(None, "fsdp")
    return jax.shard_map(
        local,
        mesh=mesh,
        in_specs=(rows, split, split, rows, columns, split, none, none, none, split, rows, rows),
        out_specs=(rows, rows, split, rows, columns, split, none, none, none, split, rows),
        check_vma=False,
    )
```

```python
import functools

import jax
import jax.numpy as jnp
import numpy as np
from jax import lax
from jax.experimental import pallas as pl
from jax.experimental.pallas import tpu as pltpu
from jax.sharding import PartitionSpec as P

HEADS = 24
HEAD_DIM = 64
STATE = 128
CONV_K = 4
INNER = HEADS * HEAD_DIM
CHANNELS = INNER + 2 * STATE
LANES = 128
CHUNK = 128
PAIRS = HEADS // 2
VMEM_BYTES = 56 * 1024 * 1024
EPS = 1e-05
FRONT = CHANNELS + LANES
FORWARD_OUTS = 9
GATE_ROW = 5
GAIN_ROW = 6
FORWARD_SPLITS = 1
BACKWARD_SPLITS = 1
F32 = jnp.float32
BF16 = jnp.bfloat16
HIGHEST = lax.Precision.HIGHEST


def mm(a, b):
    return lax.dot_general(a, b, (((1,), (0,)), ((), ())), preferred_element_type=F32)


def mm_bt(a, b):
    return lax.dot_general(a, b, (((1,), (1,)), ((), ())), preferred_element_type=F32)


def mm_at(a, b):
    return lax.dot_general(a, b, (((0,), (0,)), ((), ())), preferred_element_type=F32)


def sigmoid(x):
    return 0.5 * jnp.tanh(0.5 * x) + 0.5


def split_two(v):
    high = v.astype(BF16)
    low = (v - high.astype(F32)).astype(BF16)
    return high, low


def widen(v, spread):
    high, low = split_two(jnp.where(lane_is_head(), v, 0.0))
    packed = high.astype(F32) + pltpu.roll(low.astype(F32), 64, 1)
    return mm(packed.astype(BF16), spread)


def head_sums(v, gather):
    high, low = split_two(v)
    return mm(high, gather) + mm(low, gather)


def in_smem():
    return pl.BlockSpec(memory_space=pltpu.SMEM)


def in_vmem(count):
    return [pl.BlockSpec(memory_space=pltpu.VMEM) for _ in range(count)]


def lane_is_head():
    return lax.broadcasted_iota(jnp.int32, (1, LANES), 1) < HEADS


def triangle(kind):
    rows = lax.broadcasted_iota(jnp.int32, (CHUNK, CHUNK), 0)
    columns = lax.broadcasted_iota(jnp.int32, (CHUNK, CHUNK), 1)
    return rows >= columns if kind == "lower" else rows <= columns


def forward_kernel(
    parts_before, hidden_ref, gain_ref, w_ref, conv_ref, head_ref, skip_ref, spread_ref, tail_in, state_in, *refs
):
    refs = refs[FORWARD_OUTS * parts_before :]
    normed_ref, mixed_ref, slope_ref, convin_ref, step_ref, run_ref, sig_ref, ssd_ref, enter_ref = refs[:FORWARD_OUTS]
    tail_out, state_out, tail, state = refs[FORWARD_OUTS:]

    @pl.when(pl.program_id(0) == 0)
    def _():
        tail[0:8, :] = tail_in[...]
        state[...] = state_in[...]

    x = hidden_ref[...].astype(F32)
    scale = lax.rsqrt(jnp.mean(x * x, axis=-1, keepdims=True) + EPS)
    normed = (x * scale * gain_ref[GAIN_ROW : GAIN_ROW + 1, :]).astype(BF16)
    normed_ref[...] = normed

    conv_in = mm(normed, w_ref[:, :CHANNELS])
    convin_ref[...] = conv_in.astype(BF16)
    tail[8 : 8 + CHUNK, :] = conv_in
    conv_out = conv_ref[CONV_K : CONV_K + 1, :] + conv_ref[CONV_K - 1 : CONV_K, :] * conv_in
    for k in range(CONV_K - 1):
        conv_out = conv_out + conv_ref[k : k + 1, :] * tail[5 + k : 5 + k + CHUNK, :]
    tail[0:8, :] = tail[CHUNK : CHUNK + 8, :]
    gate = sigmoid(conv_out)
    mixed = (conv_out * gate).astype(BF16)
    mixed_ref[...] = mixed
    slope_ref[...] = (gate * (1.0 + conv_out * (1.0 - gate))).astype(BF16)

    dt = mm(normed, w_ref[:, CHANNELS:]) + head_ref[0:1, :]
    step = jnp.where(lane_is_head(), jnp.maximum(dt, 0.0) + jnp.log1p(jnp.exp(-jnp.abs(dt))), 0.0)
    step_ref[...] = step
    sig_ref[...] = sigmoid(dt)
    log_decay = -jnp.exp(head_ref[1:2, :]) * step
    lower = triangle("lower")
    run = jnp.dot(lower.astype(F32), log_decay, precision=HIGHEST, preferred_element_type=F32)
    run_ref[...] = run
    run_t = jnp.transpose(run)
    last = run[CHUNK - 1 : CHUNK, :]

    spread = spread_ref[...]
    values = mixed[:, :INNER].astype(F32)
    b_in = mixed[:, INNER : INNER + STATE]
    c_out = mixed[:, INNER + STATE :]
    scores = jnp.where(lower, mm_bt(c_out, b_in), 0.0)
    stepped = (widen(step, spread) * values).astype(BF16)
    entering = state[...]
    enter_low = entering.astype(BF16)
    enter_ref[0] = enter_low
    ssd_ref[...] = widen(jnp.exp(run), spread) * mm(c_out, enter_low) + skip_ref[...] * values
    to_end = (widen(jnp.exp(last - run), spread) * stepped.astype(F32)).astype(BF16)
    through = widen(jnp.broadcast_to(jnp.exp(last), (8, LANES)), spread)[0:1, :]
    state[...] = through * entering + mm_at(b_in, to_end)

    left_half = lax.broadcasted_iota(jnp.int32, (CHUNK, LANES), 1) < HEAD_DIM
    zero = jnp.zeros((CHUNK, LANES), BF16)
    for pair in range(PAIRS):
        mixing = []
        for h in (2 * pair, 2 * pair + 1):
            decay = jnp.exp(jnp.minimum(run[:, h : h + 1] - run_t[h : h + 1, :], 0.0))
            mixing.append((scores * decay).astype(BF16))
        both = stepped[:, pair * LANES : (pair + 1) * LANES]
        right = jnp.concatenate([jnp.where(left_half, both, zero), jnp.where(left_half, zero, both)], axis=0)
        ssd_ref[:, pair * LANES : (pair + 1) * LANES] += mm(jnp.concatenate(mixing, axis=1), right)

    @pl.when(pl.program_id(0) == pl.num_programs(0) - 1)
    def _():
        tail_out[...] = tail[0:8, :]
        state_out[...] = state[...]


def forward(hidden, gain, w, conv, head, skip_wide, spread, splits):
    rows, width = hidden.shape
    chunks = rows // CHUNK
    steps = chunks // splits
    whole = lambda a: pl.BlockSpec(a.shape, lambda i: (0,) * a.ndim)
    shapes = [
        ((rows, width), BF16), ((rows, CHANNELS), BF16), ((rows, CHANNELS), BF16), ((rows, CHANNELS), BF16),
        ((rows, LANES), F32), ((rows, LANES), F32), ((rows, LANES), F32), ((rows, INNER), F32),
        ((chunks, STATE, INNER), BF16),
    ]
    carry_shapes = [((8, CHANNELS), F32), ((STATE, INNER), F32)]
    carry = [jnp.zeros(shape, dtype) for shape, dtype in carry_shapes]
    filled = []
    flops = 2 * rows * (width * (CHANNELS + LANES) + 3 * STATE * INNER + CHUNK * INNER * 2) // splits
    for split in range(splits):
        part = lambda n, at=split * steps: pl.BlockSpec((CHUNK, n), lambda i: (at + i, 0))
        ins = (hidden, gain, w, conv, head, skip_wide, spread, *carry)
        outs = pl.pallas_call(
            functools.partial(forward_kernel, 1 if filled else 0),
            grid=(steps,),
            in_specs=[part(width)] + [whole(a) for a in ins[1:]] + [pl.BlockSpec(memory_space=pl.ANY) for _ in filled],
            out_specs=[part(shape[1]) for shape, _ in shapes[:-1]]
            + [pl.BlockSpec((1, STATE, INNER), lambda i, at=split * steps: (at + i, 0, 0))]
            + [pl.BlockSpec(shape, lambda i: (0, 0)) for shape, _ in carry_shapes],
            out_shape=[jax.ShapeDtypeStruct(shape, dtype) for shape, dtype in shapes + carry_shapes],
            scratch_shapes=[pltpu.VMEM((CHUNK + 8, CHANNELS), F32), pltpu.VMEM((STATE, INNER), F32)],
            input_output_aliases={len(ins) + k: k for k in range(len(filled))},
            compiler_params=pltpu.CompilerParams(dimension_semantics=("arbitrary",), vmem_limit_bytes=VMEM_BYTES),
            cost_estimate=pl.CostEstimate(flops=flops * 4, bytes_accessed=30_000_000 // splits, transcendentals=0),
            name="ssd_forward",
        )(*ins, *filled)
        filled, carry = list(outs[:FORWARD_OUTS]), list(outs[FORWARD_OUTS:])
    return filled


def gate_kernel(
    length_ref, normed_ref, ssd_ref, cot_ref, wz_ref, wo_ref, gg_ref,
    dz_ref, dssd_ref, no_ref, grow_ref,
):
    tile = cot_ref.shape[0]
    place = pl.program_id(0) * tile + lax.broadcasted_iota(jnp.int32, (tile, 1), 0)
    keep = (place < length_ref[0]).astype(F32)
    grow = (cot_ref[...].astype(F32) * keep).astype(BF16)
    grow_ref[...] = grow
    wo = wo_ref[...]
    gate_gain = gg_ref[GATE_ROW : GATE_ROW + 1, :]
    z = mm(normed_ref[...], wz_ref[...])
    sig = sigmoid(z)
    silu = z * sig
    ssd = ssd_ref[...]
    gated = ssd * silu
    scale = lax.rsqrt(jnp.mean(gated * gated, axis=-1, keepdims=True) + EPS)
    unit = gated * scale
    out_low = (unit * gate_gain).astype(BF16)
    no_ref[...] = out_low
    d_out = mm_bt(grow, wo)
    d_unit = d_out * gate_gain
    d_gated = scale * (d_unit - unit * jnp.mean(d_unit * unit, axis=-1, keepdims=True))
    dssd_ref[...] = (d_gated * silu).astype(BF16)
    dz_ref[...] = (d_gated * ssd * (sig * (1.0 + z * (1.0 - sig)))).astype(BF16)


def gate(lengths, normed, ssd, cot, wz, wo, gate_gain):
    rows, width = normed.shape
    tile = 256
    whole = lambda a: pl.BlockSpec(a.shape, lambda i: (0,) * a.ndim)
    part = lambda n: pl.BlockSpec((tile, n), lambda i: (i, 0))
    return pl.pallas_call(
        gate_kernel,
        grid=(rows // tile,),
        in_specs=[in_smem(), part(width), part(INNER), part(width), whole(wz), whole(wo), whole(gate_gain)],
        out_specs=[part(INNER), part(INNER), part(INNER), part(width)],
        out_shape=[
            jax.ShapeDtypeStruct((rows, INNER), BF16),
            jax.ShapeDtypeStruct((rows, INNER), BF16),
            jax.ShapeDtypeStruct((rows, INNER), BF16),
            jax.ShapeDtypeStruct((rows, width), BF16),
        ],
        compiler_params=pltpu.CompilerParams(dimension_semantics=("arbitrary",), vmem_limit_bytes=VMEM_BYTES),
        cost_estimate=pl.CostEstimate(flops=2 * rows * width * INNER * 6, bytes_accessed=30_000_000, transcendentals=0),
        name="gate_both_ways",
    )(lengths, normed, ssd, cot, wz, wo, gate_gain)


def backward_kernel(
    parts_before,
    mixed_ref, slope_ref, convin_ref, step_ref, run_ref, sig_ref, ssd_ref, enter_ref, dssd_ref,
    conv_ref, head_ref, skip_ref, spread_ref, gather_ref, ahead_in, state_in, dconvw_in, dsmall_in, dskip_in, *refs,
):
    refs = refs[2 * parts_before :]
    dconv_ref, ddt_ref, ahead_out, state_out, dconvw_ref, dsmall_ref, dskip_ref, ahead, d_state, d_values = refs

    @pl.when(pl.program_id(0) == 0)
    def _():
        ahead[CHUNK : CHUNK + 8, :] = ahead_in[...]
        d_state[...] = state_in[...]
        dconvw_ref[...] = dconvw_in[...]
        dsmall_ref[...] = dsmall_in[...]
        dskip_ref[...] = dskip_in[...]

    spread = spread_ref[...]
    gather = gather_ref[...]
    step = step_ref[...]
    run = run_ref[...]
    run_t = jnp.transpose(run)
    last = run[CHUNK - 1 : CHUNK, :]
    skip = skip_ref[...]
    mixed = mixed_ref[...]
    values = mixed[:, :INNER].astype(F32)
    b_in = mixed[:, INNER : INNER + STATE]
    c_out = mixed[:, INNER + STATE :]
    step_wide = widen(step, spread)
    end_wide = widen(jnp.exp(last - run), spread)
    stepped = (step_wide * values).astype(BF16)
    to_end = (end_wide * stepped.astype(F32)).astype(BF16)
    through = widen(jnp.broadcast_to(jnp.exp(last), (8, LANES)), spread)[0:1, :]
    d_low = dssd_ref[...]
    d_ssd = d_low.astype(F32)
    scaled = (widen(jnp.exp(run), spread) * d_ssd).astype(BF16)
    entering = enter_ref[0]
    d_leave = d_state[...]
    d_leave_low = d_leave.astype(BF16)
    upper = triangle("upper")
    scores_t = jnp.where(upper, mm_bt(b_in, c_out), 0.0)

    left_half = lax.broadcasted_iota(jnp.int32, (CHUNK, LANES), 1) < HEAD_DIM
    zero = jnp.zeros((CHUNK, LANES), BF16)
    d_scores_t = jnp.zeros((CHUNK, CHUNK), F32)
    for pair in range(PAIRS):
        lanes = slice(pair * LANES, (pair + 1) * LANES)
        d_pair = d_low[:, lanes]
        x_pair = stepped[:, lanes]
        d_split = jnp.concatenate([jnp.where(left_half, d_pair, zero), jnp.where(left_half, zero, d_pair)], axis=0)
        d_mixing = mm_bt(x_pair, d_split)
        mixing = []
        for slot, h in enumerate((2 * pair, 2 * pair + 1)):
            decay = jnp.exp(jnp.minimum(run_t[h : h + 1, :] - run[:, h : h + 1], 0.0))
            d_scores_t = d_scores_t + d_mixing[:, slot * CHUNK : (slot + 1) * CHUNK] * decay
            mixing.append((scores_t * decay).astype(BF16))
        d_values[:, lanes] = mm(jnp.concatenate(mixing, axis=1), d_split)

    d_scores_t = jnp.where(upper, d_scores_t, 0.0).astype(BF16)
    d_c = mm_at(d_scores_t, b_in) + mm_bt(scaled, entering)
    d_b = mm(d_scores_t, c_out) + mm_bt(to_end, d_leave_low)
    from_state = mm(b_in, d_leave_low)
    d_state[...] = through * d_leave + mm_at(c_out, scaled)

    d_stepped = d_values[...]
    state_part = to_end.astype(F32) * from_state
    ssd = ssd_ref[...]
    flow = d_ssd * (ssd - skip * values) - stepped.astype(F32) * d_stepped - state_part
    ending = jnp.sum(state_part, axis=0, keepdims=True) + through * jnp.sum(
        entering.astype(F32) * d_leave, axis=0, keepdims=True
    )
    is_last = lax.broadcasted_iota(jnp.int32, (CHUNK, 1), 0) == CHUNK - 1
    d_run = head_sums(flow + jnp.where(is_last, ending, 0.0), gather)
    d_stepped = d_stepped + end_wide * from_state
    d_step = head_sums(values * d_stepped, gather)
    dskip_ref[...] += jnp.sum(d_ssd * values, axis=0, keepdims=True)
    d_x = skip * d_ssd + step_wide * d_stepped

    rate = jnp.exp(head_ref[1:2, :])
    d_log = jnp.dot(upper.astype(F32), d_run, precision=HIGHEST, preferred_element_type=F32)
    d_step = d_step - rate * d_log
    d_dt = jnp.where(lane_is_head(), d_step * sig_ref[...], 0.0)
    ddt_ref[...] = d_dt.astype(BF16)
    dsmall_ref[0:1, :] += jnp.sum(d_dt, axis=0, keepdims=True)
    dsmall_ref[1:2, :] -= rate * jnp.sum(d_log * step, axis=0, keepdims=True)

    slope = slope_ref[...].astype(F32)
    ahead[0:CHUNK, :INNER] = d_x * slope[:, :INNER]
    ahead[0:CHUNK, INNER : INNER + STATE] = d_b * slope[:, INNER : INNER + STATE]
    ahead[0:CHUNK, INNER + STATE :] = d_c * slope[:, INNER + STATE :]
    conv_in = convin_ref[...].astype(F32)
    total = jnp.zeros((CHUNK, CHANNELS), F32)
    for k in range(CONV_K):
        moved = ahead[CONV_K - 1 - k : CONV_K - 1 - k + CHUNK, :]
        total = total + conv_ref[k : k + 1, :] * moved
        dconvw_ref[k : k + 1, :] += jnp.sum(moved * conv_in, axis=0, keepdims=True)
    dconvw_ref[CONV_K : CONV_K + 1, :] += jnp.sum(ahead[0:CHUNK, :], axis=0, keepdims=True)
    dconv_ref[...] = total.astype(BF16)
    ahead[CHUNK : CHUNK + 8, :] = ahead[0:8, :]

    @pl.when(pl.program_id(0) == pl.num_programs(0) - 1)
    def _():
        ahead_out[...] = ahead[CHUNK : CHUNK + 8, :]
        state_out[...] = d_state[...]
        dsmall_ref[2:3, :] = head_sums(jnp.broadcast_to(dskip_ref[...], (8, INNER)), gather)[0:1, :]


def backward(saved, d_ssd, conv, head, skip_wide, spread, gather, splits):
    mixed, slope, convin, step, run, sig, ssd, enter = saved
    rows = mixed.shape[0]
    chunks = rows // CHUNK
    steps = chunks // splits
    whole = lambda a: pl.BlockSpec(a.shape, lambda i: (0,) * a.ndim)
    shapes = [((rows, CHANNELS), BF16), ((rows, LANES), BF16)]
    carry_shapes = [(8, CHANNELS), (STATE, INNER), (8, CHANNELS), (8, LANES), (1, INNER)]
    carry = [jnp.zeros(shape, F32) for shape in carry_shapes]
    filled = []
    flops = 2 * rows * (5 * STATE * INNER + CHUNK * INNER * 4) // splits
    for split in range(splits):
        top = chunks - 1 - split * steps
        part = lambda n, top=top: pl.BlockSpec((CHUNK, n), lambda i: (top - i, 0))
        fixed = (conv, head, skip_wide, spread, gather, *carry)
        ins = (mixed, slope, convin, step, run, sig, ssd, enter, d_ssd, *fixed)
        outs = pl.pallas_call(
            functools.partial(backward_kernel, 1 if filled else 0),
            grid=(steps,),
            in_specs=[
                part(CHANNELS), part(CHANNELS), part(CHANNELS), part(LANES), part(LANES), part(LANES), part(INNER),
                pl.BlockSpec((1, STATE, INNER), lambda i, top=top: (top - i, 0, 0)), part(INNER),
            ] + [whole(a) for a in fixed] + [pl.BlockSpec(memory_space=pl.ANY) for _ in filled],
            out_specs=[part(CHANNELS), part(LANES)] + [pl.BlockSpec(shape, lambda i: (0, 0)) for shape in carry_shapes],
            out_shape=[jax.ShapeDtypeStruct(shape, dtype) for shape, dtype in shapes]
            + [jax.ShapeDtypeStruct(shape, F32) for shape in carry_shapes],
            scratch_shapes=[
                pltpu.VMEM((CHUNK + 8, CHANNELS), F32), pltpu.VMEM((STATE, INNER), F32), pltpu.VMEM((CHUNK, INNER), F32),
            ],
            input_output_aliases={len(ins) + k: k for k in range(len(filled))},
            compiler_params=pltpu.CompilerParams(dimension_semantics=("arbitrary",), vmem_limit_bytes=VMEM_BYTES),
            cost_estimate=pl.CostEstimate(flops=flops * 4, bytes_accessed=60_000_000 // splits, transcendentals=0),
            name="ssd_backward",
        )(*ins, *filled)
        filled, carry = list(outs[:2]), list(outs[2:])
    return filled[0], filled[1], carry[2], carry[3]


def finish_kernel(
    length_ref, hidden_ref, grow_ref, no_ref, dz_ref, dconv_ref, ddt_ref, gain_ref, wz_ref, w_ref, wo_ref, gh_ref, out_ref
):
    tile = hidden_ref.shape[0]
    place = pl.program_id(0) * tile + lax.broadcasted_iota(jnp.int32, (tile, 1), 0)
    keep = (place < length_ref[0]).astype(F32)
    x = hidden_ref[...].astype(F32)
    out_ref[...] = (keep * (x + mm(no_ref[...], wo_ref[...]))).astype(BF16)
    scale = lax.rsqrt(jnp.mean(x * x, axis=-1, keepdims=True) + EPS)
    unit = x * scale
    d_normed = mm_bt(dz_ref[...], wz_ref[...]) + mm_bt(dconv_ref[...], w_ref[:, :CHANNELS])
    d_normed = d_normed + mm_bt(ddt_ref[...], w_ref[:, CHANNELS:])
    d_unit = d_normed * gain_ref[GAIN_ROW : GAIN_ROW + 1, :]
    d_x = scale * (d_unit - unit * jnp.mean(d_unit * unit, axis=-1, keepdims=True))
    gh_ref[...] = grow_ref[...].astype(F32) + d_x


def finish(lengths, hidden, grow, out_low, dz, dconv, ddt, gain, wz, w, wo):
    rows, width = hidden.shape
    tile = 256
    whole = lambda a: pl.BlockSpec(a.shape, lambda i: (0,) * a.ndim)
    part = lambda n: pl.BlockSpec((tile, n), lambda i: (i, 0))
    return pl.pallas_call(
        finish_kernel,
        grid=(rows // tile,),
        in_specs=[in_smem(), part(width), part(width), part(INNER), part(INNER), part(CHANNELS), part(LANES)]
        + [whole(a) for a in (gain, wz, w, wo)],
        out_specs=[part(width), part(width)],
        out_shape=[jax.ShapeDtypeStruct((rows, width), F32), jax.ShapeDtypeStruct((rows, width), BF16)],
        compiler_params=pltpu.CompilerParams(dimension_semantics=("arbitrary",), vmem_limit_bytes=VMEM_BYTES),
        cost_estimate=pl.CostEstimate(flops=8 * rows * width * INNER * 3, bytes_accessed=30_000_000, transcendentals=0),
        name="input_norm_backward",
    )(lengths, hidden, grow, out_low, dz, dconv, ddt, gain, wz, w, wo)


CHIPS = 16


def rel_of(place):
    return (place >> 2) | ((place & 3) << 2)


def in_core_order(core, own, other):
    return jnp.where(core == 0, own, other), jnp.where(core == 0, other, own)


def blocks_of(refs, i):
    near, far, near_other, far_other = refs
    if i < 12:
        return near[i].astype(F32), near_other[i].astype(F32)
    return far[i - 12].astype(F32), far_other[i - 12].astype(F32)


def window(count, width, device):
    lane = lax.broadcasted_iota(jnp.int32, (1, count), 1)
    return (lane >= device * width) & (lane < (device + 1) * width)


def front_kernel(me_ref, e1, e2, f1, f2, small_map_ref, w_ref, conv_ref, gate_ref, gain_ref, smalls):
    core, chip = me_ref[0] & 1, me_ref[0] >> 1
    height = e1.shape[1]
    devices = 2 * CHIPS
    for i in range(CHIPS):
        first, second = in_core_order(core, *blocks_of((e1, e2, f1, f2), i))
        at = pl.multiple_of((rel_of(i) ^ chip) * (2 * height), 16)
        w_ref[pl.ds(at, 2 * height), :] = jnp.concatenate([first, second], axis=0).astype(BF16)
        smalls[16 * i : 16 * i + 8, :] = first[0:8, CHANNELS:]
        smalls[16 * i + 8 : 16 * i + 16, :] = second[0:8, CHANNELS:]
    low = smalls[...].astype(BF16)
    start = 0
    for ref in (conv_ref, gate_ref, gain_ref):
        count = ref.shape[1]
        table = mm(low, small_map_ref[:, start : start + count])
        start += count
        total = jnp.zeros((8, count), F32)
        for i in range(CHIPS):
            for k in range(2):
                device = (rel_of(i) ^ chip) * 2 + k
                rows = table[16 * i + 8 * k : 16 * i + 8 * k + 8, :]
                total = total + jnp.where(window(count, count // devices, device), rows, 0.0)
        ref[...] = total


def small_map(counts, devices):
    maps = []
    for count in counts:
        width = count // devices
        lane, row = np.arange(count)[None, :] % width, np.arange(LANES)[:, None]
        maps.append(lane + 64 == row)
    return jnp.asarray(np.concatenate(maps, axis=1), BF16)


def assemble_front(me, blocks, maps, width):
    devices = 2 * CHIPS
    return pl.pallas_call(
        front_kernel,
        in_specs=[in_smem()] + in_vmem(5),
        out_specs=in_vmem(4),
        out_shape=[
            jax.ShapeDtypeStruct((width, FRONT), BF16),
            jax.ShapeDtypeStruct((8, CHANNELS), F32),
            jax.ShapeDtypeStruct((8, INNER), F32),
            jax.ShapeDtypeStruct((8, width), F32),
        ],
        scratch_shapes=[pltpu.VMEM((8 * devices, LANES), F32)],
        compiler_params=pltpu.CompilerParams(vmem_limit_bytes=VMEM_BYTES),
        cost_estimate=pl.CostEstimate(flops=1_000_000_000, bytes_accessed=10_000_000, transcendentals=0),
        name="assemble_front",
    )(me, *blocks, maps)


def rest_kernel(blocks_ref, wz_ref, wo_ref):
    devices, height, width = blocks_ref.shape
    height = height // 4
    for c in range(devices // 2):
        first, second = blocks_ref[2 * c].astype(F32), blocks_ref[2 * c + 1].astype(F32)
        for half in range(2):
            rows = slice(half * height, (half + 1) * height)
            both = jnp.concatenate([first[rows], second[rows]], axis=0).astype(BF16)
            wz_ref[2 * height * c : 2 * height * (c + 1), half * width : (half + 1) * width] = both
        both = jnp.concatenate([first[2 * height :], second[2 * height :]], axis=0).astype(BF16)
        wo_ref[4 * height * c : 4 * height * (c + 1), :] = both


def assemble_rest(blocks):
    devices, height, width = blocks.shape
    split = 2
    part = lambda r, n: pl.BlockSpec((r // split, n), lambda i: (i, 0))
    return pl.pallas_call(
        rest_kernel,
        grid=(split,),
        in_specs=[pl.BlockSpec((devices // split, height, width), lambda i: (i, 0, 0))],
        out_specs=[part(width, INNER), part(INNER, width)],
        out_shape=[jax.ShapeDtypeStruct((width, INNER), BF16), jax.ShapeDtypeStruct((INNER, width), BF16)],
        compiler_params=pltpu.CompilerParams(dimension_semantics=("arbitrary",), vmem_limit_bytes=VMEM_BYTES),
        cost_estimate=pl.CostEstimate(flops=1_000_000_000, bytes_accessed=10_000_000, transcendentals=0),
        name="assemble_rest",
    )(blocks)


def grad_specs(height, columns):
    shape = (4, 2, 2, height, columns)
    spec = pl.BlockSpec((4, 1, 2, height, columns), lambda i, me: (0, i ^ (me[0] >> 4), 0, 0, 0))
    return [spec, spec], [jax.ShapeDtypeStruct(shape, BF16), jax.ShapeDtypeStruct(shape, BF16)]


def grad_slots(me_ref, keep_ref, send_ref):
    core, chip = me_ref[0] & 1, me_ref[0] >> 1
    for c in range(CHIPS // 2):
        rel = c ^ (chip & 7)
        for ref, part in ((keep_ref, core), (send_ref, 1 - core)):
            yield ref, (rel & 3, 0, rel >> 2), c, part


def grad_rest_kernel(me_ref, normed_ref, dz_ref, no_ref, grow_ref, keep_ref, send_ref, for_in, for_out):
    for_in[...] = mm_at(normed_ref[...], dz_ref[...])
    for_out[...] = mm_at(no_ref[...], grow_ref[...])
    height, width = keep_ref.shape[3] // 4, keep_ref.shape[4]
    for ref, at, c, part in grad_slots(me_ref, keep_ref, send_ref):
        rows = pl.ds(pl.multiple_of(2 * height * c + height * part, 8), height)
        ref[(*at, slice(0, height))] = for_in[rows, :width].astype(ref.dtype)
        ref[(*at, slice(height, 2 * height))] = for_in[rows, width:].astype(ref.dtype)
        rows = pl.ds(pl.multiple_of(4 * height * c + 2 * height * part, 16), 2 * height)
        ref[(*at, slice(2 * height, 4 * height))] = for_out[rows, :].astype(ref.dtype)


def grad_rest(me, normed, dz, out_low, grow):
    rows, width = normed.shape
    whole = lambda n: pl.BlockSpec((rows, n), lambda i, me: (0, 0))
    half = lambda n: pl.BlockSpec((rows, n // 2), lambda i, me: (0, i))
    out_specs, out_shape = grad_specs(width // CHIPS * 2, width)
    return pl.pallas_call(
        grad_rest_kernel,
        grid_spec=pltpu.PrefetchScalarGridSpec(
            num_scalar_prefetch=1,
            grid=(2,),
            in_specs=[half(width), whole(INNER), half(INNER), whole(width)],
            out_specs=out_specs,
            scratch_shapes=[pltpu.VMEM((width // 2, INNER), F32), pltpu.VMEM((INNER // 2, width), F32)],
        ),
        out_shape=out_shape,
        compiler_params=pltpu.CompilerParams(dimension_semantics=("arbitrary",), vmem_limit_bytes=VMEM_BYTES),
        cost_estimate=pl.CostEstimate(flops=4 * rows * width * INNER, bytes_accessed=16_000_000, transcendentals=0),
        name="grad_rest",
    )(me, normed, dz, out_low, grow)


def grad_front_kernel(me_ref, normed_ref, dconv_ref, ddt_ref, dconvw_ref, dhead_ref, small_map_ref, keep_ref, send_ref, for_in, smalls):
    devices = 2 * CHIPS

    @pl.when(pl.program_id(0) == 0)
    def _():
        sums = dconvw_ref[...]
        masked = [jnp.where(window(CHANNELS, CHANNELS // devices, d), sums, 0.0) for d in range(devices)]
        high, low = split_two(jnp.concatenate(masked, axis=0))
        few = mm_bt(high, small_map_ref[...]) + mm_bt(low, small_map_ref[...])
        heads = pltpu.roll(dhead_ref[...], HEADS, 1)
        heads = heads + pltpu.roll(heads - heads.astype(BF16).astype(F32), 3, 0)
        smalls[...] = few + jnp.concatenate([heads] * devices, axis=0)

    normed = normed_ref[...]
    for_in[:, :CHANNELS] = mm_at(normed, dconv_ref[...])
    for_in[:, CHANNELS:] = mm_at(normed, ddt_ref[...])
    height = keep_ref.shape[3]
    first = pl.program_id(0) * devices // 2
    for ref, at, c, part in grad_slots(me_ref, keep_ref, send_ref):
        rows = pl.ds(pl.multiple_of(2 * height * c + height * part, 8), height)
        ref[(*at, slice(0, height), slice(0, CHANNELS))] = for_in[rows, :CHANNELS].astype(ref.dtype)
        few = smalls[pl.ds(pl.multiple_of((first + 2 * c + part) * 8, 8), 8), :]
        few = jnp.concatenate([few, jnp.zeros((height - 8, LANES), F32)], axis=0)
        ref[(*at, slice(0, height), slice(CHANNELS, FRONT))] = (for_in[rows, CHANNELS:] + few).astype(ref.dtype)


def grad_front(me, normed, dconv, ddt, dconvw, dhead, maps):
    rows, width = normed.shape
    whole = lambda a: pl.BlockSpec(a.shape, lambda i, me: (0, 0))
    half = pl.BlockSpec((rows, width // 2), lambda i, me: (0, i))
    out_specs, out_shape = grad_specs(width // CHIPS // 2, FRONT)
    return pl.pallas_call(
        grad_front_kernel,
        grid_spec=pltpu.PrefetchScalarGridSpec(
            num_scalar_prefetch=1,
            grid=(2,),
            in_specs=[half, whole(dconv), whole(ddt), whole(dconvw), whole(dhead), pl.BlockSpec((LANES, CHANNELS), lambda i, me: (0, 0))],
            out_specs=out_specs,
            scratch_shapes=[pltpu.VMEM((width // 2, FRONT), F32), pltpu.VMEM((16 * CHIPS, LANES), F32)],
        ),
        out_shape=out_shape,
        compiler_params=pltpu.CompilerParams(dimension_semantics=("arbitrary",), vmem_limit_bytes=VMEM_BYTES),
        cost_estimate=pl.CostEstimate(flops=2 * rows * width * FRONT, bytes_accessed=14_000_000, transcendentals=0),
        name="grad_front",
    )(me, normed, dconv, ddt, dconvw, dhead, maps)


CORE, X, Y, Z1, Z2 = 1, 2, 4, 8, 16


def swap(v, offset):
    return lax.ppermute(v, "fsdp", [(i, i ^ offset) for i in range(2 * CHIPS)])


def gather_blocks(pack):
    own = jnp.stack([pack, swap(pack, Z1), swap(pack, Z2), swap(pack, Z1 | Z2)])
    near = jnp.concatenate([own, swap(own, X), swap(own, Y)])
    far = swap(own, X | Y)
    return near, far, swap(near, CORE), swap(far, CORE)


def low(v):
    return v.astype(BF16)


def high(v):
    return v.astype(F32)


def rounded(v):
    return lax.reduce_precision(v, 8, 7)


def add_four(own, came):
    return (rounded(own) + high(came[0])) + (high(came[1]) + high(came[2]))


def with_lost(total):
    first = CHANNELS + HEADS
    lost = (total - rounded(total))[..., :3, first : first + HEADS]
    edges = [(0, 0)] * (total.ndim - 2) + [(3, total.shape[-2] - 6), (first, FRONT - first - HEADS)]
    return total + jnp.pad(lost, edges)


def scatter_cores(keep, send, finer=lambda v: v):
    total = finer(high(keep) + high(swap(send, CORE)))
    return total[0], [low(total[k]) for k in (1, 2, 3)]


def scatter_planes(own, ready, finer=lambda v: v):
    total = finer(add_four(own, [swap(v, offset) for v, offset in zip(ready, (X, Y, X | Y))]))
    total = total.reshape(4, *total.shape[2:])
    return total[0], [low(total[k]) for k in (1, 2, 3)]


def scatter_z(own, ready):
    return add_four(own, [swap(v, offset) for v, offset in zip(ready, (Z1, Z2, Z1 | Z2))])


def after(values):
    return lax.optimization_barrier(values)


def contract_rows(left, right):
    return lax.dot_general(left, right, (((0,), (0,)), ((), ())), preferred_element_type=F32)


def head_maps():
    lane = np.arange(INNER)[None, :] // HEAD_DIM
    row = np.arange(LANES)[:, None]
    return jnp.asarray(lane == row % 64, BF16), jnp.asarray((lane == row).T, BF16)


def local(devices, hidden, lengths, norm_gain, in_w, conv_w, conv_b, dt_bias, a_log, skip, gate_gain, out_w, cotangent):
    by_hand = devices == 2 * CHIPS
    width = hidden.shape[1]
    spread, gather = head_maps()
    head = jnp.pad(jnp.stack([dt_bias, a_log]), ((0, 6), (0, LANES - HEADS)))
    skip_wide = jnp.repeat(skip, HEAD_DIM)[None, :]
    me = lax.axis_index("fsdp").astype(jnp.int32)[None]
    if by_hand:
        height = in_w.shape[0]
        maps = small_map((CHANNELS, INNER, width), devices)
        rows = [conv_w, conv_b[None], gate_gain[None], norm_gain[None]]
        rows = jnp.concatenate([jnp.pad(r, ((0, 0), (0, 64 - r.shape[1]))) for r in rows])
        rows = jnp.pad(rows, ((0, height - rows.shape[0]), (64 - HEADS, 0)))
        front_blocks = gather_blocks(jnp.concatenate([in_w[:, INNER:], rows], axis=1))
        rest_blocks = lax.all_gather(jnp.concatenate([in_w[:, :width], in_w[:, width:INNER], out_w]), "fsdp")
        w, conv, gate_gains, gain = assemble_front(me, front_blocks, maps, width)
    else:
        whole = functools.partial(lax.all_gather, axis_name="fsdp", tiled=True)
        full_in, wo = whole(in_w), whole(out_w)
        w, wz = jnp.pad(full_in[:, INNER:], ((0, 0), (0, LANES - HEADS))), full_in[:, :INNER]
        conv = jnp.concatenate([whole(conv_w, axis=1), whole(conv_b)[None]]).astype(F32)
        conv = jnp.pad(conv, ((0, 3), (0, 0)))
        gate_gains = jnp.broadcast_to(whole(gate_gain).astype(F32), (8, INNER))
        gain = jnp.broadcast_to(whole(norm_gain).astype(F32), (8, width))
    saved = forward(hidden, gain, w, conv, head, skip_wide, spread, FORWARD_SPLITS)
    normed, saved = saved[0], saved[1:]
    if by_hand:
        wz, wo = assemble_rest(rest_blocks)
    dz, d_ssd, out_low, grow = gate(lengths, normed, saved[6], cotangent, wz, wo, gate_gains)
    if by_hand:
        rest_own, rest_ready = scatter_cores(*grad_rest(me, normed, dz, out_low, grow))
        d_ssd, rest_ready = after((d_ssd, rest_ready))
    dconv, ddt, dconvw, dhead = backward(saved, d_ssd, conv, head, skip_wide, spread, gather, BACKWARD_SPLITS)
    if by_hand:
        rest_own, rest_ready = scatter_planes(rest_own, rest_ready)
        dconv, rest_own, rest_ready = after((dconv, rest_own, rest_ready))
        front_own, front_ready = scatter_cores(*grad_front(me, normed, dconv, ddt, dconvw, dhead, maps), with_lost)
        hidden, front_ready, rest_own, rest_ready = after((hidden, front_ready, rest_own, rest_ready))
        rest = scatter_z(rest_own, rest_ready)
        front_own, front_ready = scatter_planes(front_own, front_ready, with_lost)
        grad_hidden, block_out = finish(lengths, hidden, grow, out_low, dz, dconv, ddt, gain, wz, w, wo)
        front_own, front_ready, rest, grad_hidden = after((front_own, front_ready, rest, grad_hidden))
        front = scatter_z(front_own, front_ready)
        d_in = jnp.concatenate([rest[:height], rest[height : 2 * height], front[:, : CHANNELS + HEADS]], axis=1)
        d_out = rest[2 * height :]
        near = CHANNELS + 64
        d_conv = front[: CONV_K + 1, near : near + conv_b.shape[0]]
        d_conv_w, d_conv_b = d_conv[:CONV_K], d_conv[CONV_K]
        heads = front[:6, CHANNELS + HEADS : CHANNELS + 2 * HEADS]
        heads = heads[:3] + heads[3:]
    else:
        scatter = functools.partial(lax.psum_scatter, axis_name="fsdp", tiled=True)
        d_in = [contract_rows(normed, v) for v in (dz, dconv, ddt)]
        d_in = scatter(jnp.concatenate([d_in[0], d_in[1], d_in[2][:, :HEADS]], axis=1))
        d_out = scatter(contract_rows(out_low, grow))
        d_conv_w = scatter(dconvw[:CONV_K], scatter_dimension=1)
        d_conv_b = scatter(dconvw[CONV_K])
        heads = lax.psum(dhead, "fsdp")[:3, :HEADS]
        grad_hidden, block_out = finish(lengths, hidden, grow, out_low, dz, dconv, ddt, gain, wz, w, wo)
    d_norm = jnp.sum(in_w.astype(F32) * d_in, axis=1) / norm_gain.astype(F32)
    d_gate = jnp.sum(out_w.astype(F32) * d_out, axis=1) / gate_gain.astype(F32)
    return (block_out, grad_hidden, d_norm, d_in, d_conv_w, d_conv_b, heads[0], heads[1], heads[2], d_gate, d_out)


def solution(mesh):
    rows, split, none = P("fsdp", None), P("fsdp"), P()
    columns = P(None, "fsdp")
    return jax.shard_map(
        functools.partial(local, mesh.shape["fsdp"]),
        mesh=mesh,
        in_specs=(rows, split, split, rows, columns, split, none, none, none, split, rows, rows),
        out_specs=(rows, rows, split, rows, columns, split, none, none, none, split, rows),
        check_vma=False,
    )
```

```python
import functools

import jax
import jax.numpy as jnp
import numpy as np
from jax import lax
from jax.experimental import pallas as pl
from jax.experimental.pallas import tpu as pltpu
from jax.sharding import PartitionSpec as P

HEADS = 24
HEAD_DIM = 64
STATE = 128
CONV_K = 4
INNER = HEADS * HEAD_DIM
CHANNELS = INNER + 2 * STATE
LANES = 128
CHUNK = 128
PAIRS = HEADS // 2
SCAN_VMEM = 56 * 1024 * 1024
VMEM_BYTES = 30 * 1024 * 1024
EPS = 1e-05
FRONT = CHANNELS + LANES
GATE_ROW = 5
GAIN_ROW = 6
F32 = jnp.float32
BF16 = jnp.bfloat16
HIGHEST = lax.Precision.HIGHEST


def mm(a, b):
    return lax.dot_general(a, b, (((1,), (0,)), ((), ())), preferred_element_type=F32)


def mm_bt(a, b):
    return lax.dot_general(a, b, (((1,), (1,)), ((), ())), preferred_element_type=F32)


def mm_at(a, b):
    return lax.dot_general(a, b, (((0,), (0,)), ((), ())), preferred_element_type=F32)


def sigmoid(x):
    return 0.5 * jnp.tanh(0.5 * x) + 0.5


def split_two(v):
    high = v.astype(BF16)
    low = (v - high.astype(F32)).astype(BF16)
    return high, low


def widen(v, spread):
    high, low = split_two(jnp.where(lane_is_head(), v, 0.0))
    packed = high.astype(F32) + pltpu.roll(low.astype(F32), 64, 1)
    return mm(packed.astype(BF16), spread)


def head_sums(v, gather):
    high, low = split_two(v)
    return mm(high, gather) + mm(low, gather)


def in_smem():
    return pl.BlockSpec(memory_space=pltpu.SMEM)


def in_vmem(count):
    return [pl.BlockSpec(memory_space=pltpu.VMEM) for _ in range(count)]


def lane_is_head():
    return lax.broadcasted_iota(jnp.int32, (1, LANES), 1) < HEADS


def triangle(kind):
    rows = lax.broadcasted_iota(jnp.int32, (CHUNK, CHUNK), 0)
    columns = lax.broadcasted_iota(jnp.int32, (CHUNK, CHUNK), 1)
    return rows >= columns if kind == "lower" else rows <= columns


def forward_kernel(
    hidden_ref, gain_ref, w_ref, conv_ref, head_ref, skip_ref, spread_ref,
    normed_ref, mixed_ref, slope_ref, convin_ref, step_ref, run_ref, sig_ref, ssd_ref, enter_ref, tail, state,
):
    @pl.when(pl.program_id(0) == 0)
    def _():
        tail[0:8, :] = jnp.zeros((8, CHANNELS), F32)
        state[...] = jnp.zeros_like(state)

    x = hidden_ref[...].astype(F32)
    scale = lax.rsqrt(jnp.mean(x * x, axis=-1, keepdims=True) + EPS)
    normed = (x * scale * gain_ref[GAIN_ROW : GAIN_ROW + 1, :]).astype(BF16)
    normed_ref[...] = normed

    conv_in = mm(normed, w_ref[:, :CHANNELS])
    convin_ref[...] = conv_in.astype(BF16)
    tail[8 : 8 + CHUNK, :] = conv_in
    conv_out = conv_ref[CONV_K : CONV_K + 1, :] + conv_ref[CONV_K - 1 : CONV_K, :] * conv_in
    for k in range(CONV_K - 1):
        conv_out = conv_out + conv_ref[k : k + 1, :] * tail[5 + k : 5 + k + CHUNK, :]
    tail[0:8, :] = tail[CHUNK : CHUNK + 8, :]
    gate = sigmoid(conv_out)
    mixed = (conv_out * gate).astype(BF16)
    mixed_ref[...] = mixed
    slope_ref[...] = (gate * (1.0 + conv_out * (1.0 - gate))).astype(BF16)

    dt = mm(normed, w_ref[:, CHANNELS:]) + head_ref[0:1, :]
    step = jnp.where(lane_is_head(), jnp.maximum(dt, 0.0) + jnp.log1p(jnp.exp(-jnp.abs(dt))), 0.0)
    step_ref[...] = step
    sig_ref[...] = sigmoid(dt)
    log_decay = -jnp.exp(head_ref[1:2, :]) * step
    lower = triangle("lower")
    run = jnp.dot(lower.astype(F32), log_decay, precision=HIGHEST, preferred_element_type=F32)
    run_ref[...] = run
    run_t = jnp.transpose(run)
    last = run[CHUNK - 1 : CHUNK, :]

    spread = spread_ref[...]
    values = mixed[:, :INNER].astype(F32)
    b_in = mixed[:, INNER : INNER + STATE]
    c_out = mixed[:, INNER + STATE :]
    scores = jnp.where(lower, mm_bt(c_out, b_in), 0.0)
    stepped = (widen(step, spread) * values).astype(BF16)
    entering = state[...]
    enter_low = entering.astype(BF16)
    enter_ref[0] = enter_low
    ssd_ref[...] = widen(jnp.exp(run), spread) * mm(c_out, enter_low) + skip_ref[...] * values
    to_end = (widen(jnp.exp(last - run), spread) * stepped.astype(F32)).astype(BF16)
    through = widen(jnp.broadcast_to(jnp.exp(last), (8, LANES)), spread)[0:1, :]
    state[...] = through * entering + mm_at(b_in, to_end)

    left_half = lax.broadcasted_iota(jnp.int32, (CHUNK, LANES), 1) < HEAD_DIM
    zero = jnp.zeros((CHUNK, LANES), BF16)
    for pair in range(PAIRS):
        mixing = []
        for h in (2 * pair, 2 * pair + 1):
            decay = jnp.exp(jnp.minimum(run[:, h : h + 1] - run_t[h : h + 1, :], 0.0))
            mixing.append((scores * decay).astype(BF16))
        both = stepped[:, pair * LANES : (pair + 1) * LANES]
        right = jnp.concatenate([jnp.where(left_half, both, zero), jnp.where(left_half, zero, both)], axis=0)
        ssd_ref[:, pair * LANES : (pair + 1) * LANES] += mm(jnp.concatenate(mixing, axis=1), right)


def forward(hidden, gain, w, conv, head, skip_wide, spread):
    rows, width = hidden.shape
    chunks = rows // CHUNK
    whole = lambda a: pl.BlockSpec(a.shape, lambda i: (0,) * a.ndim)
    part = lambda n: pl.BlockSpec((CHUNK, n), lambda i: (i, 0))
    shapes = [
        ((rows, width), BF16), ((rows, CHANNELS), BF16), ((rows, CHANNELS), BF16), ((rows, CHANNELS), BF16),
        ((rows, LANES), F32), ((rows, LANES), F32), ((rows, LANES), F32), ((rows, INNER), F32),
        ((chunks, STATE, INNER), BF16),
    ]
    flops = 2 * rows * (width * (CHANNELS + LANES) + 3 * STATE * INNER + CHUNK * INNER * 2)
    ins = (hidden, gain, w, conv, head, skip_wide, spread)
    return pl.pallas_call(
        forward_kernel,
        grid=(chunks,),
        in_specs=[part(width)] + [whole(a) for a in ins[1:]],
        out_specs=[part(shape[1]) for shape, _ in shapes[:-1]] + [pl.BlockSpec((1, STATE, INNER), lambda i: (i, 0, 0))],
        out_shape=[jax.ShapeDtypeStruct(shape, dtype) for shape, dtype in shapes],
        scratch_shapes=[pltpu.VMEM((CHUNK + 8, CHANNELS), F32), pltpu.VMEM((STATE, INNER), F32)],
        compiler_params=pltpu.CompilerParams(dimension_semantics=("arbitrary",), vmem_limit_bytes=SCAN_VMEM),
        cost_estimate=pl.CostEstimate(flops=flops * 4, bytes_accessed=30_000_000, transcendentals=0),
        name="ssd_forward",
    )(*ins)


def gate_kernel(
    length_ref, normed_ref, ssd_ref, cot_ref, wz_ref, wo_ref, gg_ref,
    dz_ref, dssd_ref, no_ref, grow_ref,
):
    tile = cot_ref.shape[0]
    place = pl.program_id(0) * tile + lax.broadcasted_iota(jnp.int32, (tile, 1), 0)
    keep = (place < length_ref[0]).astype(F32)
    grow = (cot_ref[...].astype(F32) * keep).astype(BF16)
    grow_ref[...] = grow
    wo = wo_ref[...]
    gate_gain = gg_ref[GATE_ROW : GATE_ROW + 1, :]
    z = mm(normed_ref[...], wz_ref[...])
    sig = sigmoid(z)
    silu = z * sig
    ssd = ssd_ref[...]
    gated = ssd * silu
    scale = lax.rsqrt(jnp.mean(gated * gated, axis=-1, keepdims=True) + EPS)
    unit = gated * scale
    out_low = (unit * gate_gain).astype(BF16)
    no_ref[...] = out_low
    d_out = mm_bt(grow, wo)
    d_unit = d_out * gate_gain
    d_gated = scale * (d_unit - unit * jnp.mean(d_unit * unit, axis=-1, keepdims=True))
    dssd_ref[...] = (d_gated * silu).astype(BF16)
    dz_ref[...] = (d_gated * ssd * (sig * (1.0 + z * (1.0 - sig)))).astype(BF16)


def gate(lengths, normed, ssd, cot, wz, wo, gate_gain):
    rows, width = normed.shape
    tile = 256
    whole = lambda a: pl.BlockSpec(a.shape, lambda i: (0,) * a.ndim)
    part = lambda n: pl.BlockSpec((tile, n), lambda i: (i, 0))
    return pl.pallas_call(
        gate_kernel,
        grid=(rows // tile,),
        in_specs=[in_smem(), part(width), part(INNER), part(width), whole(wz), whole(wo), whole(gate_gain)],
        out_specs=[part(INNER), part(INNER), part(INNER), part(width)],
        out_shape=[
            jax.ShapeDtypeStruct((rows, INNER), BF16),
            jax.ShapeDtypeStruct((rows, INNER), BF16),
            jax.ShapeDtypeStruct((rows, INNER), BF16),
            jax.ShapeDtypeStruct((rows, width), BF16),
        ],
        compiler_params=pltpu.CompilerParams(dimension_semantics=("arbitrary",), vmem_limit_bytes=VMEM_BYTES),
        cost_estimate=pl.CostEstimate(flops=2 * rows * width * INNER * 6, bytes_accessed=30_000_000, transcendentals=0),
        name="gate_both_ways",
    )(lengths, normed, ssd, cot, wz, wo, gate_gain)


def backward_kernel(
    mixed_ref, slope_ref, convin_ref, step_ref, run_ref, sig_ref, ssd_ref, enter_ref, dssd_ref,
    conv_ref, head_ref, skip_ref, spread_ref, gather_ref,
    dconv_ref, ddt_ref, dconvw_ref, dsmall_ref, ahead, d_state, d_values, dskip_ref,
):
    @pl.when(pl.program_id(0) == 0)
    def _():
        ahead[CHUNK : CHUNK + 8, :] = jnp.zeros((8, CHANNELS), F32)
        d_state[...] = jnp.zeros_like(d_state)
        dconvw_ref[...] = jnp.zeros_like(dconvw_ref)
        dsmall_ref[...] = jnp.zeros_like(dsmall_ref)
        dskip_ref[...] = jnp.zeros_like(dskip_ref)

    spread = spread_ref[...]
    gather = gather_ref[...]
    step = step_ref[...]
    run = run_ref[...]
    run_t = jnp.transpose(run)
    last = run[CHUNK - 1 : CHUNK, :]
    skip = skip_ref[...]
    mixed = mixed_ref[...]
    values = mixed[:, :INNER].astype(F32)
    b_in = mixed[:, INNER : INNER + STATE]
    c_out = mixed[:, INNER + STATE :]
    step_wide = widen(step, spread)
    end_wide = widen(jnp.exp(last - run), spread)
    stepped = (step_wide * values).astype(BF16)
    to_end = (end_wide * stepped.astype(F32)).astype(BF16)
    through = widen(jnp.broadcast_to(jnp.exp(last), (8, LANES)), spread)[0:1, :]
    d_low = dssd_ref[...]
    d_ssd = d_low.astype(F32)
    scaled = (widen(jnp.exp(run), spread) * d_ssd).astype(BF16)
    entering = enter_ref[0]
    d_leave = d_state[...]
    d_leave_low = d_leave.astype(BF16)
    upper = triangle("upper")
    scores_t = jnp.where(upper, mm_bt(b_in, c_out), 0.0)

    left_half = lax.broadcasted_iota(jnp.int32, (CHUNK, LANES), 1) < HEAD_DIM
    zero = jnp.zeros((CHUNK, LANES), BF16)
    d_scores_t = jnp.zeros((CHUNK, CHUNK), F32)
    for pair in range(PAIRS):
        lanes = slice(pair * LANES, (pair + 1) * LANES)
        d_pair = d_low[:, lanes]
        x_pair = stepped[:, lanes]
        d_split = jnp.concatenate([jnp.where(left_half, d_pair, zero), jnp.where(left_half, zero, d_pair)], axis=0)
        d_mixing = mm_bt(x_pair, d_split)
        mixing = []
        for slot, h in enumerate((2 * pair, 2 * pair + 1)):
            decay = jnp.exp(jnp.minimum(run_t[h : h + 1, :] - run[:, h : h + 1], 0.0))
            d_scores_t = d_scores_t + d_mixing[:, slot * CHUNK : (slot + 1) * CHUNK] * decay
            mixing.append((scores_t * decay).astype(BF16))
        d_values[:, lanes] = mm(jnp.concatenate(mixing, axis=1), d_split)

    d_scores_t = jnp.where(upper, d_scores_t, 0.0).astype(BF16)
    d_c = mm_at(d_scores_t, b_in) + mm_bt(scaled, entering)
    d_b = mm(d_scores_t, c_out) + mm_bt(to_end, d_leave_low)
    from_state = mm(b_in, d_leave_low)
    d_state[...] = through * d_leave + mm_at(c_out, scaled)

    d_stepped = d_values[...]
    state_part = to_end.astype(F32) * from_state
    ssd = ssd_ref[...]
    flow = d_ssd * (ssd - skip * values) - stepped.astype(F32) * d_stepped - state_part
    ending = jnp.sum(state_part, axis=0, keepdims=True) + through * jnp.sum(
        entering.astype(F32) * d_leave, axis=0, keepdims=True
    )
    is_last = lax.broadcasted_iota(jnp.int32, (CHUNK, 1), 0) == CHUNK - 1
    d_run = head_sums(flow + jnp.where(is_last, ending, 0.0), gather)
    d_stepped = d_stepped + end_wide * from_state
    d_step = mm((values * d_stepped).astype(BF16), gather)
    dskip_ref[...] += jnp.sum(d_ssd * values, axis=0, keepdims=True)
    d_x = skip * d_ssd + step_wide * d_stepped

    rate = jnp.exp(head_ref[1:2, :])
    d_log = jnp.dot(upper.astype(F32), d_run, precision=HIGHEST, preferred_element_type=F32)
    d_step = d_step - rate * d_log
    d_dt = jnp.where(lane_is_head(), d_step * sig_ref[...], 0.0)
    ddt_ref[...] = d_dt.astype(BF16)
    dsmall_ref[0:1, :] += jnp.sum(d_dt, axis=0, keepdims=True)
    dsmall_ref[1:2, :] -= rate * jnp.sum(d_log * step, axis=0, keepdims=True)

    slope = slope_ref[...].astype(F32)
    ahead[0:CHUNK, :INNER] = d_x * slope[:, :INNER]
    ahead[0:CHUNK, INNER : INNER + STATE] = d_b * slope[:, INNER : INNER + STATE]
    ahead[0:CHUNK, INNER + STATE :] = d_c * slope[:, INNER + STATE :]
    conv_in = convin_ref[...].astype(F32)
    total = jnp.zeros((CHUNK, CHANNELS), F32)
    for k in range(CONV_K):
        moved = ahead[CONV_K - 1 - k : CONV_K - 1 - k + CHUNK, :]
        total = total + conv_ref[k : k + 1, :] * moved
        dconvw_ref[k : k + 1, :] += jnp.sum(moved * conv_in, axis=0, keepdims=True)
    dconvw_ref[CONV_K : CONV_K + 1, :] += jnp.sum(ahead[0:CHUNK, :], axis=0, keepdims=True)
    dconv_ref[...] = total.astype(BF16)
    ahead[CHUNK : CHUNK + 8, :] = ahead[0:8, :]

    @pl.when(pl.program_id(0) == pl.num_programs(0) - 1)
    def _():
        dsmall_ref[2:3, :] = head_sums(jnp.broadcast_to(dskip_ref[...], (8, INNER)), gather)[0:1, :]


def backward(saved, d_ssd, conv, head, skip_wide, spread, gather):
    mixed = saved[0]
    rows = mixed.shape[0]
    chunks = rows // CHUNK
    whole = lambda a: pl.BlockSpec(a.shape, lambda i: (0,) * a.ndim)
    part = lambda n: pl.BlockSpec((CHUNK, n), lambda i: (chunks - 1 - i, 0))
    total = lambda n: pl.BlockSpec((8, n), lambda i: (0, 0))
    fixed = (conv, head, skip_wide, spread, gather)
    flops = 2 * rows * (5 * STATE * INNER + CHUNK * INNER * 4)
    return pl.pallas_call(
        backward_kernel,
        grid=(chunks,),
        in_specs=[
            part(CHANNELS), part(CHANNELS), part(CHANNELS), part(LANES), part(LANES), part(LANES), part(INNER),
            pl.BlockSpec((1, STATE, INNER), lambda i: (chunks - 1 - i, 0, 0)), part(INNER),
        ] + [whole(a) for a in fixed],
        out_specs=[part(CHANNELS), part(LANES), total(CHANNELS), total(LANES)],
        out_shape=[
            jax.ShapeDtypeStruct((rows, CHANNELS), BF16),
            jax.ShapeDtypeStruct((rows, LANES), BF16),
            jax.ShapeDtypeStruct((8, CHANNELS), F32),
            jax.ShapeDtypeStruct((8, LANES), F32),
        ],
        scratch_shapes=[
            pltpu.VMEM((CHUNK + 8, CHANNELS), F32), pltpu.VMEM((STATE, INNER), F32), pltpu.VMEM((CHUNK, INNER), F32),
            pltpu.VMEM((1, INNER), F32),
        ],
        compiler_params=pltpu.CompilerParams(dimension_semantics=("arbitrary",), vmem_limit_bytes=SCAN_VMEM),
        cost_estimate=pl.CostEstimate(flops=flops * 4, bytes_accessed=60_000_000, transcendentals=0),
        name="ssd_backward",
    )(*saved, d_ssd, *fixed)


def finish_kernel(
    length_ref, hidden_ref, grow_ref, no_ref, dz_ref, dconv_ref, ddt_ref, gain_ref, wz_ref, w_ref, wo_ref, gh_ref, out_ref
):
    tile = hidden_ref.shape[0]
    place = pl.program_id(0) * tile + lax.broadcasted_iota(jnp.int32, (tile, 1), 0)
    keep = (place < length_ref[0]).astype(F32)
    x = hidden_ref[...].astype(F32)
    out_ref[...] = (keep * (x + mm(no_ref[...], wo_ref[...]))).astype(BF16)
    scale = lax.rsqrt(jnp.mean(x * x, axis=-1, keepdims=True) + EPS)
    unit = x * scale
    d_normed = mm_bt(dz_ref[...], wz_ref[...]) + mm_bt(dconv_ref[...], w_ref[:, :CHANNELS])
    d_normed = d_normed + mm_bt(ddt_ref[...], w_ref[:, CHANNELS:])
    d_unit = d_normed * gain_ref[GAIN_ROW : GAIN_ROW + 1, :]
    d_x = scale * (d_unit - unit * jnp.mean(d_unit * unit, axis=-1, keepdims=True))
    gh_ref[...] = grow_ref[...].astype(F32) + d_x


def finish(lengths, hidden, grow, out_low, dz, dconv, ddt, gain, wz, w, wo):
    rows, width = hidden.shape
    tile = 256
    whole = lambda a: pl.BlockSpec(a.shape, lambda i: (0,) * a.ndim)
    part = lambda n: pl.BlockSpec((tile, n), lambda i: (i, 0))
    return pl.pallas_call(
        finish_kernel,
        grid=(rows // tile,),
        in_specs=[in_smem(), part(width), part(width), part(INNER), part(INNER), part(CHANNELS), part(LANES)]
        + [whole(a) for a in (gain, wz, w, wo)],
        out_specs=[part(width), part(width)],
        out_shape=[jax.ShapeDtypeStruct((rows, width), F32), jax.ShapeDtypeStruct((rows, width), BF16)],
        compiler_params=pltpu.CompilerParams(dimension_semantics=("arbitrary",), vmem_limit_bytes=VMEM_BYTES),
        cost_estimate=pl.CostEstimate(flops=8 * rows * width * INNER * 3, bytes_accessed=30_000_000, transcendentals=0),
        name="input_norm_backward",
    )(lengths, hidden, grow, out_low, dz, dconv, ddt, gain, wz, w, wo)


CHIPS = 16


def rel_of(place):
    return (place >> 2) | ((place & 3) << 2)


def in_core_order(core, own, other):
    return jnp.where(core == 0, own, other), jnp.where(core == 0, other, own)


def blocks_of(refs, i):
    near, far, near_other, far_other = refs
    if i < 12:
        return near[i].astype(F32), near_other[i].astype(F32)
    return far[i - 12].astype(F32), far_other[i - 12].astype(F32)


def window(count, width, device):
    lane = lax.broadcasted_iota(jnp.int32, (1, count), 1)
    return (lane >= device * width) & (lane < (device + 1) * width)


def front_kernel(me_ref, e1, e2, f1, f2, small_map_ref, w_ref, conv_ref, gate_ref, gain_ref, smalls):
    core, chip = me_ref[0] & 1, me_ref[0] >> 1
    height = e1.shape[1]
    devices = 2 * CHIPS
    for i in range(CHIPS):
        first, second = in_core_order(core, *blocks_of((e1, e2, f1, f2), i))
        at = pl.multiple_of((rel_of(i) ^ chip) * (2 * height), 16)
        w_ref[pl.ds(at, 2 * height), :] = jnp.concatenate([first, second], axis=0).astype(BF16)
        smalls[16 * i : 16 * i + 8, :] = first[0:8, CHANNELS:]
        smalls[16 * i + 8 : 16 * i + 16, :] = second[0:8, CHANNELS:]
    low = smalls[...].astype(BF16)
    start = 0
    for ref in (conv_ref, gate_ref, gain_ref):
        count = ref.shape[1]
        table = mm(low, small_map_ref[:, start : start + count])
        start += count
        total = jnp.zeros((8, count), F32)
        for i in range(CHIPS):
            for k in range(2):
                device = (rel_of(i) ^ chip) * 2 + k
                rows = table[16 * i + 8 * k : 16 * i + 8 * k + 8, :]
                total = total + jnp.where(window(count, count // devices, device), rows, 0.0)
        ref[...] = total


def small_map(counts, devices):
    maps = []
    for count in counts:
        width = count // devices
        lane, row = np.arange(count)[None, :] % width, np.arange(LANES)[:, None]
        maps.append(lane + 64 == row)
    return jnp.asarray(np.concatenate(maps, axis=1), BF16)


def assemble_front(me, blocks, maps, width):
    devices = 2 * CHIPS
    return pl.pallas_call(
        front_kernel,
        in_specs=[in_smem()] + in_vmem(5),
        out_specs=in_vmem(4),
        out_shape=[
            jax.ShapeDtypeStruct((width, FRONT), BF16),
            jax.ShapeDtypeStruct((8, CHANNELS), F32),
            jax.ShapeDtypeStruct((8, INNER), F32),
            jax.ShapeDtypeStruct((8, width), F32),
        ],
        scratch_shapes=[pltpu.VMEM((8 * devices, LANES), F32)],
        compiler_params=pltpu.CompilerParams(vmem_limit_bytes=VMEM_BYTES),
        cost_estimate=pl.CostEstimate(flops=1_000_000_000, bytes_accessed=10_000_000, transcendentals=0),
        name="assemble_front",
    )(me, *blocks, maps)


def rest_kernel(blocks_ref, wz_ref, wo_ref):
    devices, height, width = blocks_ref.shape
    height = height // 4
    for c in range(devices // 2):
        first, second = blocks_ref[2 * c].astype(F32), blocks_ref[2 * c + 1].astype(F32)
        for half in range(2):
            rows = slice(half * height, (half + 1) * height)
            both = jnp.concatenate([first[rows], second[rows]], axis=0).astype(BF16)
            wz_ref[2 * height * c : 2 * height * (c + 1), half * width : (half + 1) * width] = both
        both = jnp.concatenate([first[2 * height :], second[2 * height :]], axis=0).astype(BF16)
        wo_ref[4 * height * c : 4 * height * (c + 1), :] = both


def assemble_rest(blocks):
    devices, height, width = blocks.shape
    split = 2
    part = lambda r, n: pl.BlockSpec((r // split, n), lambda i: (i, 0))
    return pl.pallas_call(
        rest_kernel,
        grid=(split,),
        in_specs=[pl.BlockSpec((devices // split, height, width), lambda i: (i, 0, 0))],
        out_specs=[part(width, INNER), part(INNER, width)],
        out_shape=[jax.ShapeDtypeStruct((width, INNER), BF16), jax.ShapeDtypeStruct((INNER, width), BF16)],
        compiler_params=pltpu.CompilerParams(dimension_semantics=("arbitrary",), vmem_limit_bytes=VMEM_BYTES),
        cost_estimate=pl.CostEstimate(flops=1_000_000_000, bytes_accessed=10_000_000, transcendentals=0),
        name="assemble_rest",
    )(blocks)


def grad_specs(height, columns):
    shape = (4, 2, 2, height, columns)
    spec = pl.BlockSpec((4, 1, 2, height, columns), lambda i, me: (0, i ^ (me[0] >> 4), 0, 0, 0))
    return [spec, spec], [jax.ShapeDtypeStruct(shape, BF16), jax.ShapeDtypeStruct(shape, BF16)]


def grad_slots(me_ref, keep_ref, send_ref):
    core, chip = me_ref[0] & 1, me_ref[0] >> 1
    for c in range(CHIPS // 2):
        rel = c ^ (chip & 7)
        for ref, part in ((keep_ref, core), (send_ref, 1 - core)):
            yield ref, (rel & 3, 0, rel >> 2), c, part


def grad_rest_kernel(me_ref, normed_ref, dz_ref, no_ref, grow_ref, keep_ref, send_ref, for_in, for_out):
    for_in[...] = mm_at(normed_ref[...], dz_ref[...])
    for_out[...] = mm_at(no_ref[...], grow_ref[...])
    height, width = keep_ref.shape[3] // 4, keep_ref.shape[4]
    for ref, at, c, part in grad_slots(me_ref, keep_ref, send_ref):
        rows = pl.ds(pl.multiple_of(2 * height * c + height * part, 8), height)
        ref[(*at, slice(0, height))] = for_in[rows, :width].astype(ref.dtype)
        ref[(*at, slice(height, 2 * height))] = for_in[rows, width:].astype(ref.dtype)
        rows = pl.ds(pl.multiple_of(4 * height * c + 2 * height * part, 16), 2 * height)
        ref[(*at, slice(2 * height, 4 * height))] = for_out[rows, :].astype(ref.dtype)


def grad_rest(me, normed, dz, out_low, grow):
    rows, width = normed.shape
    whole = lambda n: pl.BlockSpec((rows, n), lambda i, me: (0, 0))
    half = lambda n: pl.BlockSpec((rows, n // 2), lambda i, me: (0, i))
    out_specs, out_shape = grad_specs(width // CHIPS * 2, width)
    return pl.pallas_call(
        grad_rest_kernel,
        grid_spec=pltpu.PrefetchScalarGridSpec(
            num_scalar_prefetch=1,
            grid=(2,),
            in_specs=[half(width), whole(INNER), half(INNER), whole(width)],
            out_specs=out_specs,
            scratch_shapes=[pltpu.VMEM((width // 2, INNER), F32), pltpu.VMEM((INNER // 2, width), F32)],
        ),
        out_shape=out_shape,
        compiler_params=pltpu.CompilerParams(dimension_semantics=("arbitrary",), vmem_limit_bytes=VMEM_BYTES),
        cost_estimate=pl.CostEstimate(flops=4 * rows * width * INNER, bytes_accessed=16_000_000, transcendentals=0),
        name="grad_rest",
    )(me, normed, dz, out_low, grow)


def grad_front_kernel(me_ref, normed_ref, dconv_ref, ddt_ref, dconvw_ref, dhead_ref, small_map_ref, keep_ref, send_ref, for_in, smalls):
    devices = 2 * CHIPS

    @pl.when(pl.program_id(0) == 0)
    def _():
        sums = dconvw_ref[...]
        masked = [jnp.where(window(CHANNELS, CHANNELS // devices, d), sums, 0.0) for d in range(devices)]
        high, low = split_two(jnp.concatenate(masked, axis=0))
        few = mm_bt(high, small_map_ref[...]) + mm_bt(low, small_map_ref[...])
        heads = pltpu.roll(dhead_ref[...], HEADS, 1)
        heads = heads + pltpu.roll(heads - heads.astype(BF16).astype(F32), 3, 0)
        smalls[...] = few + jnp.concatenate([heads] * devices, axis=0)

    normed = normed_ref[...]
    for_in[:, :CHANNELS] = mm_at(normed, dconv_ref[...])
    for_in[:, CHANNELS:] = mm_at(normed, ddt_ref[...])
    height = keep_ref.shape[3]
    first = pl.program_id(0) * devices // 2
    for ref, at, c, part in grad_slots(me_ref, keep_ref, send_ref):
        rows = pl.ds(pl.multiple_of(2 * height * c + height * part, 8), height)
        ref[(*at, slice(0, height), slice(0, CHANNELS))] = for_in[rows, :CHANNELS].astype(ref.dtype)
        few = smalls[pl.ds(pl.multiple_of((first + 2 * c + part) * 8, 8), 8), :]
        few = jnp.concatenate([few, jnp.zeros((height - 8, LANES), F32)], axis=0)
        ref[(*at, slice(0, height), slice(CHANNELS, FRONT))] = (for_in[rows, CHANNELS:] + few).astype(ref.dtype)


def grad_front(me, normed, dconv, ddt, dconvw, dhead, maps):
    rows, width = normed.shape
    whole = lambda a: pl.BlockSpec(a.shape, lambda i, me: (0, 0))
    half = pl.BlockSpec((rows, width // 2), lambda i, me: (0, i))
    out_specs, out_shape = grad_specs(width // CHIPS // 2, FRONT)
    return pl.pallas_call(
        grad_front_kernel,
        grid_spec=pltpu.PrefetchScalarGridSpec(
            num_scalar_prefetch=1,
            grid=(2,),
            in_specs=[half, whole(dconv), whole(ddt), whole(dconvw), whole(dhead), pl.BlockSpec((LANES, CHANNELS), lambda i, me: (0, 0))],
            out_specs=out_specs,
            scratch_shapes=[pltpu.VMEM((width // 2, FRONT), F32), pltpu.VMEM((16 * CHIPS, LANES), F32)],
        ),
        out_shape=out_shape,
        compiler_params=pltpu.CompilerParams(dimension_semantics=("arbitrary",), vmem_limit_bytes=VMEM_BYTES),
        cost_estimate=pl.CostEstimate(flops=2 * rows * width * FRONT, bytes_accessed=14_000_000, transcendentals=0),
        name="grad_front",
    )(me, normed, dconv, ddt, dconvw, dhead, maps)


CORE, X, Y, Z1, Z2 = 1, 2, 4, 8, 16


def swap(v, offset):
    return lax.ppermute(v, "fsdp", [(i, i ^ offset) for i in range(2 * CHIPS)])


def gather_blocks(pack):
    own = jnp.stack([pack, swap(pack, Z1), swap(pack, Z2), swap(pack, Z1 | Z2)])
    near = jnp.concatenate([own, swap(own, X), swap(own, Y)])
    far = swap(own, X | Y)
    return near, far, swap(near, CORE), swap(far, CORE)


def low(v):
    return v.astype(BF16)


def high(v):
    return v.astype(F32)


def rounded(v):
    return lax.reduce_precision(v, 8, 7)


def add_four(own, came):
    return (rounded(own) + high(came[0])) + (high(came[1]) + high(came[2]))


def with_lost(total):
    first = CHANNELS + HEADS
    lost = (total - rounded(total))[..., :3, first : first + HEADS]
    edges = [(0, 0)] * (total.ndim - 2) + [(3, total.shape[-2] - 6), (first, FRONT - first - HEADS)]
    return total + jnp.pad(lost, edges)


def scatter_cores(keep, send, finer=lambda v: v):
    total = finer(high(keep) + high(swap(send, CORE)))
    return total[0], [low(total[k]) for k in (1, 2, 3)]


def scatter_planes(own, ready, finer=lambda v: v):
    total = finer(add_four(own, [swap(v, offset) for v, offset in zip(ready, (X, Y, X | Y))]))
    total = total.reshape(4, *total.shape[2:])
    return total[0], [low(total[k]) for k in (1, 2, 3)]


def scatter_z(own, ready):
    return add_four(own, [swap(v, offset) for v, offset in zip(ready, (Z1, Z2, Z1 | Z2))])


def after(values):
    return lax.optimization_barrier(values)


def contract_rows(left, right):
    return lax.dot_general(left, right, (((0,), (0,)), ((), ())), preferred_element_type=F32)


def head_maps():
    lane = np.arange(INNER)[None, :] // HEAD_DIM
    row = np.arange(LANES)[:, None]
    return jnp.asarray(lane == row % 64, BF16), jnp.asarray((lane == row).T, BF16)


def local(devices, hidden, lengths, norm_gain, in_w, conv_w, conv_b, dt_bias, a_log, skip, gate_gain, out_w, cotangent):
    by_hand = devices == 2 * CHIPS
    width = hidden.shape[1]
    spread, gather = head_maps()
    head = jnp.pad(jnp.stack([dt_bias, a_log]), ((0, 6), (0, LANES - HEADS)))
    skip_wide = jnp.repeat(skip, HEAD_DIM)[None, :]
    me = lax.axis_index("fsdp").astype(jnp.int32)[None]
    if by_hand:
        height = in_w.shape[0]
        maps = small_map((CHANNELS, INNER, width), devices)
        rows = [conv_w, conv_b[None], gate_gain[None], norm_gain[None]]
        rows = jnp.concatenate([jnp.pad(r, ((0, 0), (0, 64 - r.shape[1]))) for r in rows])
        rows = jnp.pad(rows, ((0, height - rows.shape[0]), (64 - HEADS, 0)))
        front_blocks = gather_blocks(jnp.concatenate([in_w[:, INNER:], rows], axis=1))
        rest_blocks = lax.all_gather(jnp.concatenate([in_w[:, :width], in_w[:, width:INNER], out_w]), "fsdp")
        w, conv, gate_gains, gain = assemble_front(me, front_blocks, maps, width)
    else:
        whole = functools.partial(lax.all_gather, axis_name="fsdp", tiled=True)
        full_in, wo = whole(in_w), whole(out_w)
        w, wz = jnp.pad(full_in[:, INNER:], ((0, 0), (0, LANES - HEADS))), full_in[:, :INNER]
        conv = jnp.concatenate([whole(conv_w, axis=1), whole(conv_b)[None]]).astype(F32)
        conv = jnp.pad(conv, ((0, 3), (0, 0)))
        gate_gains = jnp.broadcast_to(whole(gate_gain).astype(F32), (8, INNER))
        gain = jnp.broadcast_to(whole(norm_gain).astype(F32), (8, width))
    saved = forward(hidden, gain, w, conv, head, skip_wide, spread)
    normed, saved = saved[0], saved[1:]
    if by_hand:
        wz, wo = assemble_rest(rest_blocks)
    dz, d_ssd, out_low, grow = gate(lengths, normed, saved[6], cotangent, wz, wo, gate_gains)
    if by_hand:
        rest_own, rest_ready = scatter_cores(*grad_rest(me, normed, dz, out_low, grow))
        d_ssd, rest_ready = after((d_ssd, rest_ready))
    dconv, ddt, dconvw, dhead = backward(saved, d_ssd, conv, head, skip_wide, spread, gather)
    if by_hand:
        rest_own, rest_ready = scatter_planes(rest_own, rest_ready)
        dconv, rest_own, rest_ready = after((dconv, rest_own, rest_ready))
        front_own, front_ready = scatter_cores(*grad_front(me, normed, dconv, ddt, dconvw, dhead, maps), with_lost)
        hidden, front_ready, rest_own, rest_ready = after((hidden, front_ready, rest_own, rest_ready))
        rest = scatter_z(rest_own, rest_ready)
        front_own, front_ready = scatter_planes(front_own, front_ready, with_lost)
        grad_hidden, block_out = finish(lengths, hidden, grow, out_low, dz, dconv, ddt, gain, wz, w, wo)
        front_own, front_ready, rest, grad_hidden = after((front_own, front_ready, rest, grad_hidden))
        front = scatter_z(front_own, front_ready)
        d_in = jnp.concatenate([rest[:height], rest[height : 2 * height], front[:, : CHANNELS + HEADS]], axis=1)
        d_out = rest[2 * height :]
        near = CHANNELS + 64
        d_conv = front[: CONV_K + 1, near : near + conv_b.shape[0]]
        d_conv_w, d_conv_b = d_conv[:CONV_K], d_conv[CONV_K]
        heads = front[:6, CHANNELS + HEADS : CHANNELS + 2 * HEADS]
        heads = heads[:3] + heads[3:]
    else:
        scatter = functools.partial(lax.psum_scatter, axis_name="fsdp", tiled=True)
        d_in = [contract_rows(normed, v) for v in (dz, dconv, ddt)]
        d_in = scatter(jnp.concatenate([d_in[0], d_in[1], d_in[2][:, :HEADS]], axis=1))
        d_out = scatter(contract_rows(out_low, grow))
        d_conv_w = scatter(dconvw[:CONV_K], scatter_dimension=1)
        d_conv_b = scatter(dconvw[CONV_K])
        heads = lax.psum(dhead, "fsdp")[:3, :HEADS]
        grad_hidden, block_out = finish(lengths, hidden, grow, out_low, dz, dconv, ddt, gain, wz, w, wo)
    d_norm = jnp.sum(in_w.astype(F32) * d_in, axis=1) / norm_gain.astype(F32)
    d_gate = jnp.sum(out_w.astype(F32) * d_out, axis=1) / gate_gain.astype(F32)
    return (block_out, grad_hidden, d_norm, d_in, d_conv_w, d_conv_b, heads[0], heads[1], heads[2], d_gate, d_out)


def solution(mesh):
    rows, split, none = P("fsdp", None), P("fsdp"), P()
    columns = P(None, "fsdp")
    return jax.shard_map(
        functools.partial(local, mesh.shape["fsdp"]),
        mesh=mesh,
        in_specs=(rows, split, split, rows, columns, split, none, none, none, split, rows, rows),
        out_specs=(rows, rows, split, rows, columns, split, none, none, none, split, rows),
        check_vma=False,
    )
```

```python
import functools

import jax
import jax.numpy as jnp
import numpy as np
from jax import lax
from jax.experimental import pallas as pl
from jax.experimental.pallas import tpu as pltpu
from jax.sharding import PartitionSpec as P

HEADS = 24
HEAD_DIM = 64
STATE = 128
CONV_K = 4
INNER = HEADS * HEAD_DIM
CHANNELS = INNER + 2 * STATE
LANES = 128
CHUNK = 128
PAIRS = HEADS // 2
SCAN_VMEM = 44 * 1024 * 1024
VMEM_BYTES = 30 * 1024 * 1024
EPS = 1e-05
FRONT = CHANNELS + LANES
GATE_ROW = 5
GAIN_ROW = 6
F32 = jnp.float32
BF16 = jnp.bfloat16
HIGHEST = lax.Precision.HIGHEST


def mm(a, b):
    return lax.dot_general(a, b, (((1,), (0,)), ((), ())), preferred_element_type=F32)


def mm_bt(a, b):
    return lax.dot_general(a, b, (((1,), (1,)), ((), ())), preferred_element_type=F32)


def mm_at(a, b):
    return lax.dot_general(a, b, (((0,), (0,)), ((), ())), preferred_element_type=F32)


def sigmoid(x):
    return 0.5 * jnp.tanh(0.5 * x) + 0.5


def split_two(v):
    high = v.astype(BF16)
    low = (v - high.astype(F32)).astype(BF16)
    return high, low


def widen(v, spread):
    high, low = split_two(jnp.where(lane_is_head(), v, 0.0))
    packed = high.astype(F32) + pltpu.roll(low.astype(F32), 64, 1)
    return mm(packed.astype(BF16), spread)


def head_sums(v, gather):
    high, low = split_two(v)
    return mm(high, gather) + mm(low, gather)


def in_smem():
    return pl.BlockSpec(memory_space=pltpu.SMEM)


def in_vmem(count):
    return [pl.BlockSpec(memory_space=pltpu.VMEM) for _ in range(count)]


def lane_is_head():
    return lax.broadcasted_iota(jnp.int32, (1, LANES), 1) < HEADS


def triangle(kind):
    rows = lax.broadcasted_iota(jnp.int32, (CHUNK, CHUNK), 0)
    columns = lax.broadcasted_iota(jnp.int32, (CHUNK, CHUNK), 1)
    return rows >= columns if kind == "lower" else rows <= columns


def forward_kernel(
    hidden_ref, gain_ref, w_ref, conv_ref, head_ref, skip_ref, spread_ref,
    normed_ref, mixed_ref, slope_ref, convin_ref, step_ref, run_ref, sig_ref, ssd_ref, enter_ref, tail, state,
):
    @pl.when(pl.program_id(0) == 0)
    def _():
        tail[0:8, :] = jnp.zeros((8, CHANNELS), F32)
        state[...] = jnp.zeros_like(state)

    x = hidden_ref[...].astype(F32)
    scale = lax.rsqrt(jnp.mean(x * x, axis=-1, keepdims=True) + EPS)
    normed = (x * scale * gain_ref[GAIN_ROW : GAIN_ROW + 1, :]).astype(BF16)
    normed_ref[...] = normed

    conv_in = mm(normed, w_ref[:, :CHANNELS])
    convin_ref[...] = conv_in.astype(BF16)
    tail[8 : 8 + CHUNK, :] = conv_in
    conv_out = conv_ref[CONV_K : CONV_K + 1, :] + conv_ref[CONV_K - 1 : CONV_K, :] * conv_in
    for k in range(CONV_K - 1):
        conv_out = conv_out + conv_ref[k : k + 1, :] * tail[5 + k : 5 + k + CHUNK, :]
    tail[0:8, :] = tail[CHUNK : CHUNK + 8, :]
    gate = sigmoid(conv_out)
    mixed = (conv_out * gate).astype(BF16)
    mixed_ref[...] = mixed
    slope_ref[...] = (gate * (1.0 + conv_out * (1.0 - gate))).astype(BF16)

    dt = mm(normed, w_ref[:, CHANNELS:]) + head_ref[0:1, :]
    step = jnp.where(lane_is_head(), jnp.maximum(dt, 0.0) + jnp.log1p(jnp.exp(-jnp.abs(dt))), 0.0)
    step_ref[...] = step
    sig_ref[...] = sigmoid(dt)
    log_decay = -jnp.exp(head_ref[1:2, :]) * step
    lower = triangle("lower")
    run = jnp.dot(lower.astype(F32), log_decay, precision=HIGHEST, preferred_element_type=F32)
    run_ref[...] = run
    run_t = jnp.transpose(run)
    last = run[CHUNK - 1 : CHUNK, :]

    spread = spread_ref[...]
    values = mixed[:, :INNER].astype(F32)
    b_in = mixed[:, INNER : INNER + STATE]
    c_out = mixed[:, INNER + STATE :]
    scores = jnp.where(lower, mm_bt(c_out, b_in), 0.0)
    stepped = (widen(step, spread) * values).astype(BF16)
    entering = state[...]
    enter_low = entering.astype(BF16)
    enter_ref[0] = enter_low
    ssd_ref[...] = widen(jnp.exp(run), spread) * mm(c_out, enter_low) + skip_ref[...] * values
    to_end = (widen(jnp.exp(last - run), spread) * stepped.astype(F32)).astype(BF16)
    through = widen(jnp.broadcast_to(jnp.exp(last), (8, LANES)), spread)[0:1, :]
    state[...] = through * entering + mm_at(b_in, to_end)

    left_half = lax.broadcasted_iota(jnp.int32, (CHUNK, LANES), 1) < HEAD_DIM
    zero = jnp.zeros((CHUNK, LANES), BF16)
    for pair in range(PAIRS):
        mixing = []
        for h in (2 * pair, 2 * pair + 1):
            decay = jnp.exp(jnp.minimum(run[:, h : h + 1] - run_t[h : h + 1, :], 0.0))
            mixing.append((scores * decay).astype(BF16))
        both = stepped[:, pair * LANES : (pair + 1) * LANES]
        right = jnp.concatenate([jnp.where(left_half, both, zero), jnp.where(left_half, zero, both)], axis=0)
        ssd_ref[:, pair * LANES : (pair + 1) * LANES] += mm(jnp.concatenate(mixing, axis=1), right)


def forward(hidden, gain, w, conv, head, skip_wide, spread):
    rows, width = hidden.shape
    chunks = rows // CHUNK
    whole = lambda a: pl.BlockSpec(a.shape, lambda i: (0,) * a.ndim)
    part = lambda n: pl.BlockSpec((CHUNK, n), lambda i: (i, 0))
    shapes = [
        ((rows, width), BF16), ((rows, CHANNELS), BF16), ((rows, CHANNELS), BF16), ((rows, CHANNELS), BF16),
        ((rows, LANES), F32), ((rows, LANES), F32), ((rows, LANES), F32), ((rows, INNER), F32),
        ((chunks, STATE, INNER), BF16),
    ]
    flops = 2 * rows * (width * (CHANNELS + LANES) + 3 * STATE * INNER + CHUNK * INNER * 2)
    ins = (hidden, gain, w, conv, head, skip_wide, spread)
    return pl.pallas_call(
        forward_kernel,
        grid=(chunks,),
        in_specs=[part(width)] + [whole(a) for a in ins[1:]],
        out_specs=[part(shape[1]) for shape, _ in shapes[:-1]] + [pl.BlockSpec((1, STATE, INNER), lambda i: (i, 0, 0))],
        out_shape=[jax.ShapeDtypeStruct(shape, dtype) for shape, dtype in shapes],
        scratch_shapes=[pltpu.VMEM((CHUNK + 8, CHANNELS), F32), pltpu.VMEM((STATE, INNER), F32)],
        compiler_params=pltpu.CompilerParams(dimension_semantics=("arbitrary",), vmem_limit_bytes=SCAN_VMEM),
        cost_estimate=pl.CostEstimate(flops=flops * 4, bytes_accessed=30_000_000, transcendentals=0),
        name="ssd_forward",
    )(*ins)


def gate_kernel(
    length_ref, normed_ref, ssd_ref, cot_ref, wz_ref, wo_ref, gg_ref,
    dz_ref, dssd_ref, no_ref, grow_ref,
):
    tile = cot_ref.shape[0]
    place = pl.program_id(0) * tile + lax.broadcasted_iota(jnp.int32, (tile, 1), 0)
    keep = (place < length_ref[0]).astype(F32)
    grow = (cot_ref[...].astype(F32) * keep).astype(BF16)
    grow_ref[...] = grow
    wo = wo_ref[...]
    gate_gain = gg_ref[GATE_ROW : GATE_ROW + 1, :]
    z = mm(normed_ref[...], wz_ref[...])
    sig = sigmoid(z)
    silu = z * sig
    ssd = ssd_ref[...]
    gated = ssd * silu
    scale = lax.rsqrt(jnp.mean(gated * gated, axis=-1, keepdims=True) + EPS)
    unit = gated * scale
    out_low = (unit * gate_gain).astype(BF16)
    no_ref[...] = out_low
    d_out = mm_bt(grow, wo)
    d_unit = d_out * gate_gain
    d_gated = scale * (d_unit - unit * jnp.mean(d_unit * unit, axis=-1, keepdims=True))
    dssd_ref[...] = (d_gated * silu).astype(BF16)
    dz_ref[...] = (d_gated * ssd * (sig * (1.0 + z * (1.0 - sig)))).astype(BF16)


def gate(lengths, normed, ssd, cot, wz, wo, gate_gain):
    rows, width = normed.shape
    tile = 256
    whole = lambda a: pl.BlockSpec(a.shape, lambda i: (0,) * a.ndim)
    part = lambda n: pl.BlockSpec((tile, n), lambda i: (i, 0))
    return pl.pallas_call(
        gate_kernel,
        grid=(rows // tile,),
        in_specs=[in_smem(), part(width), part(INNER), part(width), whole(wz), whole(wo), whole(gate_gain)],
        out_specs=[part(INNER), part(INNER), part(INNER), part(width)],
        out_shape=[
            jax.ShapeDtypeStruct((rows, INNER), BF16),
            jax.ShapeDtypeStruct((rows, INNER), BF16),
            jax.ShapeDtypeStruct((rows, INNER), BF16),
            jax.ShapeDtypeStruct((rows, width), BF16),
        ],
        compiler_params=pltpu.CompilerParams(dimension_semantics=("arbitrary",), vmem_limit_bytes=VMEM_BYTES),
        cost_estimate=pl.CostEstimate(flops=2 * rows * width * INNER * 6, bytes_accessed=30_000_000, transcendentals=0),
        name="gate_both_ways",
    )(lengths, normed, ssd, cot, wz, wo, gate_gain)


def backward_kernel(
    mixed_ref, slope_ref, convin_ref, step_ref, run_ref, sig_ref, ssd_ref, enter_ref, dssd_ref,
    conv_ref, head_ref, skip_ref, spread_ref, gather_ref,
    dconv_ref, ddt_ref, dconvw_ref, dsmall_ref, ahead, d_state, d_values, dskip_ref,
):
    @pl.when(pl.program_id(0) == 0)
    def _():
        ahead[CHUNK : CHUNK + 8, :] = jnp.zeros((8, CHANNELS), F32)
        d_state[...] = jnp.zeros_like(d_state)
        dconvw_ref[...] = jnp.zeros_like(dconvw_ref)
        dsmall_ref[...] = jnp.zeros_like(dsmall_ref)
        dskip_ref[...] = jnp.zeros_like(dskip_ref)

    spread = spread_ref[...]
    gather = gather_ref[...]
    step = step_ref[...]
    run = run_ref[...]
    run_t = jnp.transpose(run)
    last = run[CHUNK - 1 : CHUNK, :]
    skip = skip_ref[...]
    mixed = mixed_ref[...]
    values = mixed[:, :INNER].astype(F32)
    b_in = mixed[:, INNER : INNER + STATE]
    c_out = mixed[:, INNER + STATE :]
    step_wide = widen(step, spread)
    end_wide = widen(jnp.exp(last - run), spread)
    stepped = (step_wide * values).astype(BF16)
    to_end = (end_wide * stepped.astype(F32)).astype(BF16)
    through = widen(jnp.broadcast_to(jnp.exp(last), (8, LANES)), spread)[0:1, :]
    d_low = dssd_ref[...]
    d_ssd = d_low.astype(F32)
    scaled = (widen(jnp.exp(run), spread) * d_ssd).astype(BF16)
    entering = enter_ref[0]
    d_leave = d_state[...]
    d_leave_low = d_leave.astype(BF16)
    upper = triangle("upper")
    scores_t = jnp.where(upper, mm_bt(b_in, c_out), 0.0)

    left_half = lax.broadcasted_iota(jnp.int32, (CHUNK, LANES), 1) < HEAD_DIM
    zero = jnp.zeros((CHUNK, LANES), BF16)
    d_scores_t = jnp.zeros((CHUNK, CHUNK), F32)
    for pair in range(PAIRS):
        lanes = slice(pair * LANES, (pair + 1) * LANES)
        d_pair = d_low[:, lanes]
        x_pair = stepped[:, lanes]
        d_split = jnp.concatenate([jnp.where(left_half, d_pair, zero), jnp.where(left_half, zero, d_pair)], axis=0)
        d_mixing = mm_bt(x_pair, d_split)
        mixing = []
        for slot, h in enumerate((2 * pair, 2 * pair + 1)):
            decay = jnp.exp(jnp.minimum(run_t[h : h + 1, :] - run[:, h : h + 1], 0.0))
            d_scores_t = d_scores_t + d_mixing[:, slot * CHUNK : (slot + 1) * CHUNK] * decay
            mixing.append((scores_t * decay).astype(BF16))
        d_values[:, lanes] = mm(jnp.concatenate(mixing, axis=1), d_split)

    d_scores_t = jnp.where(upper, d_scores_t, 0.0).astype(BF16)
    d_c = mm_at(d_scores_t, b_in) + mm_bt(scaled, entering)
    d_b = mm(d_scores_t, c_out) + mm_bt(to_end, d_leave_low)
    from_state = mm(b_in, d_leave_low)
    d_state[...] = through * d_leave + mm_at(c_out, scaled)

    d_stepped = d_values[...]
    state_part = to_end.astype(F32) * from_state
    ssd = ssd_ref[...]
    flow = d_ssd * (ssd - skip * values) - stepped.astype(F32) * d_stepped - state_part
    ending = jnp.sum(state_part, axis=0, keepdims=True) + through * jnp.sum(
        entering.astype(F32) * d_leave, axis=0, keepdims=True
    )
    is_last = lax.broadcasted_iota(jnp.int32, (CHUNK, 1), 0) == CHUNK - 1
    d_run = head_sums(flow + jnp.where(is_last, ending, 0.0), gather)
    d_stepped = d_stepped + end_wide * from_state
    d_step = mm((values * d_stepped).astype(BF16), gather)
    dskip_ref[...] += jnp.sum(d_ssd * values, axis=0, keepdims=True)
    d_x = skip * d_ssd + step_wide * d_stepped

    rate = jnp.exp(head_ref[1:2, :])
    d_log = jnp.dot(upper.astype(F32), d_run, precision=HIGHEST, preferred_element_type=F32)
    d_step = d_step - rate * d_log
    d_dt = jnp.where(lane_is_head(), d_step * sig_ref[...], 0.0)
    ddt_ref[...] = d_dt.astype(BF16)
    dsmall_ref[0:1, :] += jnp.sum(d_dt, axis=0, keepdims=True)
    dsmall_ref[1:2, :] -= rate * jnp.sum(d_log * step, axis=0, keepdims=True)

    slope = slope_ref[...].astype(F32)
    ahead[0:CHUNK, :INNER] = d_x * slope[:, :INNER]
    ahead[0:CHUNK, INNER : INNER + STATE] = d_b * slope[:, INNER : INNER + STATE]
    ahead[0:CHUNK, INNER + STATE :] = d_c * slope[:, INNER + STATE :]
    conv_in = convin_ref[...].astype(F32)
    total = jnp.zeros((CHUNK, CHANNELS), F32)
    for k in range(CONV_K):
        moved = ahead[CONV_K - 1 - k : CONV_K - 1 - k + CHUNK, :]
        total = total + conv_ref[k : k + 1, :] * moved
        dconvw_ref[k : k + 1, :] += jnp.sum(moved * conv_in, axis=0, keepdims=True)
    dconvw_ref[CONV_K : CONV_K + 1, :] += jnp.sum(ahead[0:CHUNK, :], axis=0, keepdims=True)
    dconv_ref[...] = total.astype(BF16)
    ahead[CHUNK : CHUNK + 8, :] = ahead[0:8, :]

    @pl.when(pl.program_id(0) == pl.num_programs(0) - 1)
    def _():
        dsmall_ref[2:3, :] = head_sums(jnp.broadcast_to(dskip_ref[...], (8, INNER)), gather)[0:1, :]


def backward(saved, d_ssd, conv, head, skip_wide, spread, gather):
    mixed = saved[0]
    rows = mixed.shape[0]
    chunks = rows // CHUNK
    whole = lambda a: pl.BlockSpec(a.shape, lambda i: (0,) * a.ndim)
    part = lambda n: pl.BlockSpec((CHUNK, n), lambda i: (chunks - 1 - i, 0))
    total = lambda n: pl.BlockSpec((8, n), lambda i: (0, 0))
    fixed = (conv, head, skip_wide, spread, gather)
    flops = 2 * rows * (5 * STATE * INNER + CHUNK * INNER * 4)
    return pl.pallas_call(
        backward_kernel,
        grid=(chunks,),
        in_specs=[
            part(CHANNELS), part(CHANNELS), part(CHANNELS), part(LANES), part(LANES), part(LANES), part(INNER),
            pl.BlockSpec((1, STATE, INNER), lambda i: (chunks - 1 - i, 0, 0)), part(INNER),
        ] + [whole(a) for a in fixed],
        out_specs=[part(CHANNELS), part(LANES), total(CHANNELS), total(LANES)],
        out_shape=[
            jax.ShapeDtypeStruct((rows, CHANNELS), BF16),
            jax.ShapeDtypeStruct((rows, LANES), BF16),
            jax.ShapeDtypeStruct((8, CHANNELS), F32),
            jax.ShapeDtypeStruct((8, LANES), F32),
        ],
        scratch_shapes=[
            pltpu.VMEM((CHUNK + 8, CHANNELS), F32), pltpu.VMEM((STATE, INNER), F32), pltpu.VMEM((CHUNK, INNER), F32),
            pltpu.VMEM((1, INNER), F32),
        ],
        compiler_params=pltpu.CompilerParams(dimension_semantics=("arbitrary",), vmem_limit_bytes=SCAN_VMEM),
        cost_estimate=pl.CostEstimate(flops=flops * 4, bytes_accessed=60_000_000, transcendentals=0),
        name="ssd_backward",
    )(*saved, d_ssd, *fixed)


def finish_kernel(
    length_ref, hidden_ref, grow_ref, no_ref, dz_ref, dconv_ref, ddt_ref, gain_ref, wz_ref, w_ref, wo_ref, gh_ref, out_ref
):
    tile = hidden_ref.shape[0]
    place = pl.program_id(0) * tile + lax.broadcasted_iota(jnp.int32, (tile, 1), 0)
    keep = (place < length_ref[0]).astype(F32)
    x = hidden_ref[...].astype(F32)
    out_ref[...] = (keep * (x + mm(no_ref[...], wo_ref[...]))).astype(BF16)
    scale = lax.rsqrt(jnp.mean(x * x, axis=-1, keepdims=True) + EPS)
    unit = x * scale
    d_normed = mm_bt(dz_ref[...], wz_ref[...]) + mm_bt(dconv_ref[...], w_ref[:, :CHANNELS])
    d_normed = d_normed + mm_bt(ddt_ref[...], w_ref[:, CHANNELS:])
    d_unit = d_normed * gain_ref[GAIN_ROW : GAIN_ROW + 1, :]
    d_x = scale * (d_unit - unit * jnp.mean(d_unit * unit, axis=-1, keepdims=True))
    gh_ref[...] = grow_ref[...].astype(F32) + d_x


def finish(lengths, hidden, grow, out_low, dz, dconv, ddt, gain, wz, w, wo):
    rows, width = hidden.shape
    tile = 256
    whole = lambda a: pl.BlockSpec(a.shape, lambda i: (0,) * a.ndim)
    part = lambda n: pl.BlockSpec((tile, n), lambda i: (i, 0))
    return pl.pallas_call(
        finish_kernel,
        grid=(rows // tile,),
        in_specs=[in_smem(), part(width), part(width), part(INNER), part(INNER), part(CHANNELS), part(LANES)]
        + [whole(a) for a in (gain, wz, w, wo)],
        out_specs=[part(width), part(width)],
        out_shape=[jax.ShapeDtypeStruct((rows, width), F32), jax.ShapeDtypeStruct((rows, width), BF16)],
        compiler_params=pltpu.CompilerParams(dimension_semantics=("arbitrary",), vmem_limit_bytes=VMEM_BYTES),
        cost_estimate=pl.CostEstimate(flops=8 * rows * width * INNER * 3, bytes_accessed=30_000_000, transcendentals=0),
        name="input_norm_backward",
    )(lengths, hidden, grow, out_low, dz, dconv, ddt, gain, wz, w, wo)


CHIPS = 16


def rel_of(place):
    return (place >> 2) | ((place & 3) << 2)


def in_core_order(core, own, other):
    return jnp.where(core == 0, own, other), jnp.where(core == 0, other, own)


def blocks_of(refs, i):
    near, far, near_other, far_other = refs
    if i < 12:
        return near[i].astype(F32), near_other[i].astype(F32)
    return far[i - 12].astype(F32), far_other[i - 12].astype(F32)


def window(count, width, device):
    lane = lax.broadcasted_iota(jnp.int32, (1, count), 1)
    return (lane >= device * width) & (lane < (device + 1) * width)


def front_kernel(me_ref, e1, e2, f1, f2, small_map_ref, w_ref, conv_ref, gate_ref, gain_ref, smalls):
    core, chip = me_ref[0] & 1, me_ref[0] >> 1
    height = e1.shape[1]
    devices = 2 * CHIPS
    for i in range(CHIPS):
        first, second = in_core_order(core, *blocks_of((e1, e2, f1, f2), i))
        at = pl.multiple_of((rel_of(i) ^ chip) * (2 * height), 16)
        w_ref[pl.ds(at, 2 * height), :] = jnp.concatenate([first, second], axis=0).astype(BF16)
        smalls[16 * i : 16 * i + 8, :] = first[0:8, CHANNELS:]
        smalls[16 * i + 8 : 16 * i + 16, :] = second[0:8, CHANNELS:]
    low = smalls[...].astype(BF16)
    start = 0
    for ref in (conv_ref, gate_ref, gain_ref):
        count = ref.shape[1]
        table = mm(low, small_map_ref[:, start : start + count])
        start += count
        total = jnp.zeros((8, count), F32)
        for i in range(CHIPS):
            for k in range(2):
                device = (rel_of(i) ^ chip) * 2 + k
                rows = table[16 * i + 8 * k : 16 * i + 8 * k + 8, :]
                total = total + jnp.where(window(count, count // devices, device), rows, 0.0)
        ref[...] = total


def small_map(counts, devices):
    maps = []
    for count in counts:
        width = count // devices
        lane, row = np.arange(count)[None, :] % width, np.arange(LANES)[:, None]
        maps.append(lane + 64 == row)
    return jnp.asarray(np.concatenate(maps, axis=1), BF16)


def assemble_front(me, blocks, maps, width):
    devices = 2 * CHIPS
    return pl.pallas_call(
        front_kernel,
        in_specs=[in_smem()] + in_vmem(5),
        out_specs=in_vmem(4),
        out_shape=[
            jax.ShapeDtypeStruct((width, FRONT), BF16),
            jax.ShapeDtypeStruct((8, CHANNELS), F32),
            jax.ShapeDtypeStruct((8, INNER), F32),
            jax.ShapeDtypeStruct((8, width), F32),
        ],
        scratch_shapes=[pltpu.VMEM((8 * devices, LANES), F32)],
        compiler_params=pltpu.CompilerParams(vmem_limit_bytes=VMEM_BYTES),
        cost_estimate=pl.CostEstimate(flops=1_000_000_000, bytes_accessed=10_000_000, transcendentals=0),
        name="assemble_front",
    )(me, *blocks, maps)


def rest_kernel(blocks_ref, wz_ref, wo_ref):
    devices, height, width = blocks_ref.shape
    height = height // 4
    for c in range(devices // 2):
        first, second = blocks_ref[2 * c].astype(F32), blocks_ref[2 * c + 1].astype(F32)
        for half in range(2):
            rows = slice(half * height, (half + 1) * height)
            both = jnp.concatenate([first[rows], second[rows]], axis=0).astype(BF16)
            wz_ref[2 * height * c : 2 * height * (c + 1), half * width : (half + 1) * width] = both
        both = jnp.concatenate([first[2 * height :], second[2 * height :]], axis=0).astype(BF16)
        wo_ref[4 * height * c : 4 * height * (c + 1), :] = both


def assemble_rest(blocks):
    devices, height, width = blocks.shape
    split = 2
    part = lambda r, n: pl.BlockSpec((r // split, n), lambda i: (i, 0))
    return pl.pallas_call(
        rest_kernel,
        grid=(split,),
        in_specs=[pl.BlockSpec((devices // split, height, width), lambda i: (i, 0, 0))],
        out_specs=[part(width, INNER), part(INNER, width)],
        out_shape=[jax.ShapeDtypeStruct((width, INNER), BF16), jax.ShapeDtypeStruct((INNER, width), BF16)],
        compiler_params=pltpu.CompilerParams(dimension_semantics=("arbitrary",), vmem_limit_bytes=VMEM_BYTES),
        cost_estimate=pl.CostEstimate(flops=1_000_000_000, bytes_accessed=10_000_000, transcendentals=0),
        name="assemble_rest",
    )(blocks)


def grad_specs(height, columns):
    shape = (4, 2, 2, height, columns)
    spec = pl.BlockSpec((4, 1, 2, height, columns), lambda i, me: (0, i ^ (me[0] >> 4), 0, 0, 0))
    return [spec, spec], [jax.ShapeDtypeStruct(shape, BF16), jax.ShapeDtypeStruct(shape, BF16)]


def grad_slots(me_ref, keep_ref, send_ref):
    core, chip = me_ref[0] & 1, me_ref[0] >> 1
    for c in range(CHIPS // 2):
        rel = c ^ (chip & 7)
        for ref, part in ((keep_ref, core), (send_ref, 1 - core)):
            yield ref, (rel & 3, 0, rel >> 2), c, part


def grad_rest_kernel(me_ref, normed_ref, dz_ref, no_ref, grow_ref, keep_ref, send_ref, for_in, for_out):
    for_in[...] = mm_at(normed_ref[...], dz_ref[...])
    for_out[...] = mm_at(no_ref[...], grow_ref[...])
    height, width = keep_ref.shape[3] // 4, keep_ref.shape[4]
    for ref, at, c, part in grad_slots(me_ref, keep_ref, send_ref):
        rows = pl.ds(pl.multiple_of(2 * height * c + height * part, 8), height)
        ref[(*at, slice(0, height))] = for_in[rows, :width].astype(ref.dtype)
        ref[(*at, slice(height, 2 * height))] = for_in[rows, width:].astype(ref.dtype)
        rows = pl.ds(pl.multiple_of(4 * height * c + 2 * height * part, 16), 2 * height)
        ref[(*at, slice(2 * height, 4 * height))] = for_out[rows, :].astype(ref.dtype)


def grad_rest(me, normed, dz, out_low, grow):
    rows, width = normed.shape
    whole = lambda n: pl.BlockSpec((rows, n), lambda i, me: (0, 0))
    half = lambda n: pl.BlockSpec((rows, n // 2), lambda i, me: (0, i))
    out_specs, out_shape = grad_specs(width // CHIPS * 2, width)
    return pl.pallas_call(
        grad_rest_kernel,
        grid_spec=pltpu.PrefetchScalarGridSpec(
            num_scalar_prefetch=1,
            grid=(2,),
            in_specs=[half(width), whole(INNER), half(INNER), whole(width)],
            out_specs=out_specs,
            scratch_shapes=[pltpu.VMEM((width // 2, INNER), F32), pltpu.VMEM((INNER // 2, width), F32)],
        ),
        out_shape=out_shape,
        compiler_params=pltpu.CompilerParams(dimension_semantics=("arbitrary",), vmem_limit_bytes=VMEM_BYTES),
        cost_estimate=pl.CostEstimate(flops=4 * rows * width * INNER, bytes_accessed=16_000_000, transcendentals=0),
        name="grad_rest",
    )(me, normed, dz, out_low, grow)


def grad_front_kernel(me_ref, normed_ref, dconv_ref, ddt_ref, dconvw_ref, dhead_ref, small_map_ref, keep_ref, send_ref, for_in, smalls):
    devices = 2 * CHIPS

    @pl.when(pl.program_id(0) == 0)
    def _():
        sums = dconvw_ref[...]
        masked = [jnp.where(window(CHANNELS, CHANNELS // devices, d), sums, 0.0) for d in range(devices)]
        high, low = split_two(jnp.concatenate(masked, axis=0))
        few = mm_bt(high, small_map_ref[...]) + mm_bt(low, small_map_ref[...])
        heads = pltpu.roll(dhead_ref[...], HEADS, 1)
        heads = heads + pltpu.roll(heads - heads.astype(BF16).astype(F32), 3, 0)
        smalls[...] = few + jnp.concatenate([heads] * devices, axis=0)

    normed = normed_ref[...]
    for_in[:, :CHANNELS] = mm_at(normed, dconv_ref[...])
    for_in[:, CHANNELS:] = mm_at(normed, ddt_ref[...])
    height = keep_ref.shape[3]
    first = pl.program_id(0) * devices // 2
    for ref, at, c, part in grad_slots(me_ref, keep_ref, send_ref):
        rows = pl.ds(pl.multiple_of(2 * height * c + height * part, 8), height)
        ref[(*at, slice(0, height), slice(0, CHANNELS))] = for_in[rows, :CHANNELS].astype(ref.dtype)
        few = smalls[pl.ds(pl.multiple_of((first + 2 * c + part) * 8, 8), 8), :]
        few = jnp.concatenate([few, jnp.zeros((height - 8, LANES), F32)], axis=0)
        ref[(*at, slice(0, height), slice(CHANNELS, FRONT))] = (for_in[rows, CHANNELS:] + few).astype(ref.dtype)


def grad_front(me, normed, dconv, ddt, dconvw, dhead, maps):
    rows, width = normed.shape
    whole = lambda a: pl.BlockSpec(a.shape, lambda i, me: (0, 0))
    half = pl.BlockSpec((rows, width // 2), lambda i, me: (0, i))
    out_specs, out_shape = grad_specs(width // CHIPS // 2, FRONT)
    return pl.pallas_call(
        grad_front_kernel,
        grid_spec=pltpu.PrefetchScalarGridSpec(
            num_scalar_prefetch=1,
            grid=(2,),
            in_specs=[half, whole(dconv), whole(ddt), whole(dconvw), whole(dhead), pl.BlockSpec((LANES, CHANNELS), lambda i, me: (0, 0))],
            out_specs=out_specs,
            scratch_shapes=[pltpu.VMEM((width // 2, FRONT), F32), pltpu.VMEM((16 * CHIPS, LANES), F32)],
        ),
        out_shape=out_shape,
        compiler_params=pltpu.CompilerParams(dimension_semantics=("arbitrary",), vmem_limit_bytes=VMEM_BYTES),
        cost_estimate=pl.CostEstimate(flops=2 * rows * width * FRONT, bytes_accessed=14_000_000, transcendentals=0),
        name="grad_front",
    )(me, normed, dconv, ddt, dconvw, dhead, maps)


CORE, X, Y, Z1, Z2 = 1, 2, 4, 8, 16


def swap(v, offset):
    return lax.ppermute(v, "fsdp", [(i, i ^ offset) for i in range(2 * CHIPS)])


def gather_blocks(pack, beside_it):
    own = jnp.stack([pack, swap(pack, Z1), swap(pack, Z2), swap(pack, Z1 | Z2)])
    own, *beside_it = after((own, *beside_it))
    beside, above = swap(own, X), swap(own, Y)
    near = jnp.concatenate([own, beside, above])
    far = jnp.concatenate([swap(beside[:2], Y), swap(above[2:], X)])
    return (near, far, swap(near, CORE), swap(far, CORE)), beside_it


def low(v):
    return v.astype(BF16)


def high(v):
    return v.astype(F32)


def rounded(v):
    return lax.reduce_precision(v, 8, 7)


def add_four(own, came):
    return (rounded(own) + high(came[0])) + (high(came[1]) + high(came[2]))


def with_lost(total):
    first = CHANNELS + HEADS
    lost = (total - rounded(total))[..., :3, first : first + HEADS]
    edges = [(0, 0)] * (total.ndim - 2) + [(3, total.shape[-2] - 6), (first, FRONT - first - HEADS)]
    return total + jnp.pad(lost, edges)


def scatter_cores(keep, send, finer=lambda v: v):
    total = finer(high(keep) + high(swap(send, CORE)))
    return total[0], [low(total[k]) for k in (1, 2, 3)]


def scatter_planes(own, ready, finer=lambda v: v):
    total = finer(add_four(own, [swap(v, offset) for v, offset in zip(ready, (X, Y, X | Y))]))
    total = total.reshape(4, *total.shape[2:])
    return total[0], [low(total[k]) for k in (1, 2, 3)]


def scatter_z(own, ready):
    return add_four(own, [swap(v, offset) for v, offset in zip(ready, (Z1, Z2, Z1 | Z2))])


def after(values):
    return lax.optimization_barrier(values)


def contract_rows(left, right):
    return lax.dot_general(left, right, (((0,), (0,)), ((), ())), preferred_element_type=F32)


def head_maps():
    lane = np.arange(INNER)[None, :] // HEAD_DIM
    row = np.arange(LANES)[:, None]
    return jnp.asarray(lane == row % 64, BF16), jnp.asarray((lane == row).T, BF16)


def local(devices, hidden, lengths, norm_gain, in_w, conv_w, conv_b, dt_bias, a_log, skip, gate_gain, out_w, cotangent):
    by_hand = devices == 2 * CHIPS
    width = hidden.shape[1]
    spread, gather = head_maps()
    head = jnp.pad(jnp.stack([dt_bias, a_log]), ((0, 6), (0, LANES - HEADS)))
    skip_wide = jnp.repeat(skip, HEAD_DIM)[None, :]
    in_scaled = in_w.astype(F32) / norm_gain.astype(F32)[:, None]
    out_scaled = out_w.astype(F32) / gate_gain.astype(F32)[:, None]
    me = lax.axis_index("fsdp").astype(jnp.int32)[None]
    if by_hand:
        height = in_w.shape[0]
        maps = small_map((CHANNELS, INNER, width), devices)
        rows = [conv_w, conv_b[None], gate_gain[None], norm_gain[None]]
        rows = jnp.concatenate([jnp.pad(r, ((0, 0), (0, 64 - r.shape[1]))) for r in rows])
        rows = jnp.pad(rows, ((0, height - rows.shape[0]), (64 - HEADS, 0)))
        pack = jnp.concatenate([in_w[:, INNER:], rows], axis=1)
        front_blocks, (head, skip_wide, in_scaled, out_scaled) = gather_blocks(pack, (head, skip_wide, in_scaled, out_scaled))
        rest_blocks = lax.all_gather(jnp.concatenate([in_w[:, :width], in_w[:, width:INNER], out_w]), "fsdp")
        w, conv, gate_gains, gain = assemble_front(me, front_blocks, maps, width)
    else:
        whole = functools.partial(lax.all_gather, axis_name="fsdp", tiled=True)
        full_in, wo = whole(in_w), whole(out_w)
        w, wz = jnp.pad(full_in[:, INNER:], ((0, 0), (0, LANES - HEADS))), full_in[:, :INNER]
        conv = jnp.concatenate([whole(conv_w, axis=1), whole(conv_b)[None]]).astype(F32)
        conv = jnp.pad(conv, ((0, 3), (0, 0)))
        gate_gains = jnp.broadcast_to(whole(gate_gain).astype(F32), (8, INNER))
        gain = jnp.broadcast_to(whole(norm_gain).astype(F32), (8, width))
    saved = forward(hidden, gain, w, conv, head, skip_wide, spread)
    normed, saved = saved[0], saved[1:]
    if by_hand:
        wz, wo = assemble_rest(rest_blocks)
    dz, d_ssd, out_low, grow = gate(lengths, normed, saved[6], cotangent, wz, wo, gate_gains)
    if by_hand:
        rest_own, rest_ready = scatter_cores(*grad_rest(me, normed, dz, out_low, grow))
        d_ssd, rest_ready = after((d_ssd, rest_ready))
    dconv, ddt, dconvw, dhead = backward(saved, d_ssd, conv, head, skip_wide, spread, gather)
    if by_hand:
        rest_own, rest_ready = scatter_planes(rest_own, rest_ready)
        dconv, rest_own, rest_ready = after((dconv, rest_own, rest_ready))
        front_own, front_ready = scatter_cores(*grad_front(me, normed, dconv, ddt, dconvw, dhead, maps), with_lost)
        hidden, front_ready, rest_own, rest_ready = after((hidden, front_ready, rest_own, rest_ready))
        rest = scatter_z(rest_own, rest_ready)
        front_own, front_ready = scatter_planes(front_own, front_ready, with_lost)
        grad_hidden, block_out = finish(lengths, hidden, grow, out_low, dz, dconv, ddt, gain, wz, w, wo)
        front_own, front_ready, rest, grad_hidden = after((front_own, front_ready, rest, grad_hidden))
        front = scatter_z(front_own, front_ready)
        d_in = jnp.concatenate([rest[:height], rest[height : 2 * height], front[:, : CHANNELS + HEADS]], axis=1)
        d_out = rest[2 * height :]
        near = CHANNELS + 64
        d_conv = front[: CONV_K + 1, near : near + conv_b.shape[0]]
        d_conv_w, d_conv_b = d_conv[:CONV_K], d_conv[CONV_K]
        heads = front[:6, CHANNELS + HEADS : CHANNELS + 2 * HEADS]
        heads = heads[:3] + heads[3:]
    else:
        scatter = functools.partial(lax.psum_scatter, axis_name="fsdp", tiled=True)
        d_in = [contract_rows(normed, v) for v in (dz, dconv, ddt)]
        d_in = scatter(jnp.concatenate([d_in[0], d_in[1], d_in[2][:, :HEADS]], axis=1))
        d_out = scatter(contract_rows(out_low, grow))
        d_conv_w = scatter(dconvw[:CONV_K], scatter_dimension=1)
        d_conv_b = scatter(dconvw[CONV_K])
        heads = lax.psum(dhead, "fsdp")[:3, :HEADS]
        grad_hidden, block_out = finish(lengths, hidden, grow, out_low, dz, dconv, ddt, gain, wz, w, wo)
    d_norm = jnp.sum(in_scaled * d_in, axis=1)
    d_gate = jnp.sum(out_scaled * d_out, axis=1)
    return (block_out, grad_hidden, d_norm, d_in, d_conv_w, d_conv_b, heads[0], heads[1], heads[2], d_gate, d_out)


def solution(mesh):
    rows, split, none = P("fsdp", None), P("fsdp"), P()
    columns = P(None, "fsdp")
    return jax.shard_map(
        functools.partial(local, mesh.shape["fsdp"]),
        mesh=mesh,
        in_specs=(rows, split, split, rows, columns, split, none, none, none, split, rows, rows),
        out_specs=(rows, rows, split, rows, columns, split, none, none, none, split, rows),
        check_vma=False,
    )
```
